512 devices in a mesh: blk: 32 (over y, x, core), qsub: 16 (over z).
Axes of the slice: x: 4, y: 4, z: 16, core: 2. Of those that a mesh axis runs over, the one named last changes fastest.
Arguments:
- queries: bfloat16 [196608, 128], P(('blk', 'qsub')), may hold values from -6 to 6
- key_rows: bfloat16 [196608, 128], P('blk'), may hold values from -6 to 6
- log_norms: bfloat16 [196608], P(('blk', 'qsub')), may hold values from 8 to 12
- positions: int32 [196608], P(('blk', 'qsub')), may hold values from 0 to 12287, as said below
Outputs:
- key_score: float32 [196608], P('blk')
The draws below stay inside these ranges and needn't reach their ends.
Inputs may be any that keep to these rules, and one draw needn't show every extreme that they name: positions is 0 at the first token of each document and rises by one per token within it; no document is longer than 12288 tokens and one is exactly 12288 long.
All inputs are finite; a program needn't handle non-finite values.
Results may differ from the reference program's by a relative error of at most 0.0003.
Values may be sent and summed in bfloat16 or wider, within the bound.
A program may use at most 64 MiB of HBM per device.

```python
import jax
import jax.numpy as jnp
from jax import lax

HEAD = 128
TOK_BLK = 6144
CONTEXT = 196608
LONGEST = 12288
N_BLK = 32


def draw_positions(key, part):
    key = jax.random.fold_in(key, 7)
    first_key, second_key = jax.random.split(key)
    index_all = jnp.arange(CONTEXT, dtype=jnp.int32)
    starts = jax.random.randint(first_key, (CONTEXT,), 0, TOK_BLK // 2) == 0
    starts = starts | (index_all % LONGEST == 0)
    anchor = jax.random.randint(second_key, (), 0, CONTEXT - LONGEST + 1)
    inside = (index_all > anchor) & (index_all < anchor + LONGEST)
    starts = starts & jnp.logical_not(inside) | (index_all == anchor) | (index_all == anchor + LONGEST)
    begins = lax.cummax(jnp.where(starts, index_all, 0), axis=0)
    return (index_all - begins).astype(jnp.int32)


def shard_levels(own_key, extent, shards, low, top_value):
    loudness = 1.0
    for dim, parts in shards:
        heights = jax.random.uniform(jax.random.fold_in(jax.random.fold_in(own_key, 6), dim), (parts,), jnp.float32, low / len(shards), top_value / len(shards))
        loudness = loudness * jnp.repeat(jnp.exp(heights), extent[dim] // parts).reshape((-1,) + (1,) * (len(extent) - 1 - dim))
    return loudness


def normal_values(key, shape, deviation, bound, cuts=(), kind=jnp.bfloat16):
    drawn = jax.random.normal(key, shape, jnp.float32) * deviation
    if len(cuts) > 0:
        drawn = shard_levels(key, shape, cuts, -0.22, 0.18) * drawn
    return jnp.clip(drawn, min=-bound, max=bound).astype(kind)


def setup_inputs(seed: int = 0) -> dict:
    seeds = jax.random.split(jax.random.key(seed), 5)
    return {
        "queries": normal_values(seeds[0], (CONTEXT, HEAD), 1.0, 6.0, ((0, 512),)),
        "key_rows": normal_values(seeds[1], (CONTEXT, HEAD), 1.0, 6.0, ((0, 32),)),
        "log_norms": jnp.clip(8.0 + 4.0 * jax.random.uniform(seeds[2], (CONTEXT,), jnp.float32) ** shard_levels(seeds[2], (CONTEXT,), ((0, 512),), -0.2, 0.2), 8.0, 12.0).astype(jnp.bfloat16),
        "positions": draw_positions(jax.random.fold_in(seeds[4], 71), 0),
    }


NEG = -1e30


def column_max(query_block, norm_block, row_index, lower_index, key_block):
    scores = jnp.dot(query_block, key_block.T, preferred_element_type=jnp.float32) * (HEAD ** -0.5)
    scores = scores - norm_block[:, None]
    columns = jnp.arange(key_block.shape[0], dtype=jnp.int32)
    visible = (columns[None, :] <= row_index[:, None]) & (columns[None, :] >= lower_index[:, None])
    return jnp.max(jnp.where(visible, scores, jnp.float32(NEG)), axis=0)


def reference(queries, key_rows, log_norms, positions):
    query_blocks = queries.reshape(N_BLK, TOK_BLK, HEAD)
    key_blocks = key_rows.reshape(N_BLK, TOK_BLK, HEAD)
    norm_blocks = log_norms.astype(jnp.float32).reshape(N_BLK, TOK_BLK)
    place_blocks = positions.reshape(N_BLK, TOK_BLK)
    earlier = jnp.concatenate([jnp.zeros((1, TOK_BLK, HEAD), key_rows.dtype), key_blocks[:-1]], axis=0)
    index_rows = jnp.arange(TOK_BLK, dtype=jnp.int32)

    def per_block(pieces):
        query_block, norm_block, place_block, home_keys, prior_keys = pieces
        home = column_max(query_block, norm_block, index_rows, index_rows - place_block, home_keys)
        shifted = index_rows + TOK_BLK
        prior = column_max(query_block, norm_block, shifted, shifted - place_block, prior_keys)
        return home, prior

    home, prior = lax.map(per_block, (query_blocks, norm_blocks, place_blocks, key_blocks, earlier))
    returned = jnp.concatenate([prior[1:], jnp.full((1, TOK_BLK), NEG, jnp.float32)], axis=0)
    return jnp.maximum(home, returned).reshape(CONTEXT)
```

```python
import functools

import jax
import jax.numpy as jnp
from jax import lax
from jax.experimental import pallas as pl
from jax.experimental.pallas import tpu as pltpu
from jax.sharding import PartitionSpec as P

MESH = pl.DeviceIdType.MESH
NEG = -1e30
FAR = 1e30
TILE = 256


def dot_rows(left, right):
    return lax.dot_general(left, right, (((1,), (1,)), ((), ())), preferred_element_type=jnp.float32)


def down(row):
    return jnp.transpose(jnp.broadcast_to(row, (128, row.shape[1])))


def off_diagonal(q_ref, c_ref, k_ref, first, width):
    query = q_ref[...]
    rows = query.shape[0]
    columns = c_ref[...]
    parts = []
    for tile in range(width // TILE):
        keys = k_ref[pl.ds(pl.multiple_of(first + tile * TILE, TILE), TILE), :]
        score = dot_rows(query, keys)
        score = score - jnp.concatenate([columns] * (TILE // 128), axis=1)
        parts.append(jnp.max(score, axis=0, keepdims=True))
    return jnp.concatenate(parts, axis=1)


def kernel(
    n_blk, n_z, scale,
    q_hbm, k_hbm, ln_hbm, pos_hbm, out_ref,
    q_v, k_v, ln_v, pos_v, qn_v, cs_v, cn_v, ch_col, cd_col, lo_col, cn_col,
    home_v, part_v, recv_v, own_v,
    in_sem, qs_sem, qr_sem, cs_sem, cr_sem, rs_send, rs_recv, ag_send, ag_recv, own_sem,
):
    b = lax.axis_index("blk")
    z = lax.axis_index("qsub")
    rows = q_v.shape[0]
    n_keys = k_v.shape[0]
    pair = 2 * rows
    n_pair = n_keys // pair
    before = lax.rem(b + n_blk - 1, n_blk)
    after = lax.rem(b + 1, n_blk)

    barrier = pltpu.get_barrier_semaphore()
    pl.semaphore_signal(barrier, inc=1, device_id={"blk": before}, device_id_type=MESH)
    pl.semaphore_signal(barrier, inc=1, device_id={"blk": after}, device_id_type=MESH)
    for step in range(1, n_z):
        pl.semaphore_signal(barrier, inc=1, device_id={"qsub": lax.rem(z + step, n_z)}, device_id_type=MESH)

    ins = [
        pltpu.make_async_copy(ln_hbm, ln_v, in_sem.at[0]),
        pltpu.make_async_copy(pos_hbm, pos_v, in_sem.at[1]),
        pltpu.make_async_copy(q_hbm, q_v, in_sem.at[2]),
        pltpu.make_async_copy(k_hbm, k_v, in_sem.at[3]),
    ]
    for copy in ins:
        copy.start()
    ins[0].wait()
    ins[1].wait()

    start = z * rows
    lane = lax.broadcasted_iota(jnp.int32, (1, rows), 1)
    pos = pos_v[...].reshape(1, rows)
    norm = ln_v[...].astype(jnp.float32).reshape(1, rows) * (1.0 / scale)
    first_pos = pos[:, 0:1]
    c_home = jnp.where(pos > lane, norm, FAR)
    c_next = jnp.where(pos > lane + start, norm, FAR)
    low_home = start - first_pos
    low_next = n_keys + start - first_pos
    cs_v[0:1, :] = c_next
    cs_v[1:2, :] = jnp.broadcast_to(low_next.astype(jnp.float32), (1, rows))

    pl.semaphore_wait(barrier, n_z + 1)
    send_q = pltpu.make_async_remote_copy(
        src_ref=q_hbm, dst_ref=qn_v, send_sem=qs_sem, recv_sem=qr_sem,
        device_id={"blk": before}, device_id_type=MESH)
    send_c = pltpu.make_async_remote_copy(
        src_ref=cs_v, dst_ref=cn_v, send_sem=cs_sem, recv_sem=cr_sem,
        device_id={"blk": before}, device_id_type=MESH)
    send_c.start()
    send_q.start()

    ch_col[...] = down(c_home)
    cd_col[...] = down(norm)
    lo_col[...] = down((lane - pos).astype(jnp.float32))

    home_v[...] = jnp.full(home_v.shape, NEG, jnp.float32)
    ins[2].wait()
    ins[3].wait()
    key_lane = lax.broadcasted_iota(jnp.int32, (1, pair), 1)

    def home_step(m, carry):
        best = off_diagonal(q_v, ch_col, k_v, m * pair, pair)
        j = key_lane + m * pair
        home_v[m] = jnp.where((j >= low_home) & (j < start), best, NEG)
        return carry

    lax.fori_loop(0, lax.div(z, 2) + 1, home_step, 0)

    keys = k_v[pl.ds(pl.multiple_of(start, 128), rows), :]
    score = dot_rows(q_v[...], keys)
    wide = rows // 128
    score = score - jnp.concatenate([cd_col[...]] * wide, axis=1)
    j = lax.broadcasted_iota(jnp.int32, (rows, rows), 1)
    r = lax.broadcasted_iota(jnp.int32, (rows, rows), 0)
    low = jnp.concatenate([lo_col[...]] * wide, axis=1)
    score = jnp.where((j <= r) & (j.astype(jnp.float32) >= low), score, NEG)
    own = jnp.max(score, axis=0, keepdims=True)
    own = jnp.concatenate([own, own], axis=1)
    mine = lax.div(z, 2)
    home_v[mine] = jnp.maximum(home_v[mine], jnp.where(lax.div(key_lane, rows) == lax.rem(z, 2), own, NEG))

    send_c.wait_recv()
    cn = cn_v[...]
    cn_col[...] = down(cn[0:1, :])
    low_n = jnp.where(b < n_blk - 1, cn[1:2, 0:1], jnp.float32(4 * n_keys)).astype(jnp.int32)
    send_q.wait_recv()

    def reduce_copy(p):
        return pltpu.make_async_remote_copy(
            src_ref=part_v.at[lax.div(p, 2), :, pl.ds(pl.multiple_of(lax.rem(p, 2) * rows, 128), rows)],
            dst_ref=recv_v.at[z], send_sem=rs_send.at[p], recv_sem=rs_recv.at[z],
            device_id={"qsub": p}, device_id_type=MESH)

    def next_step(t, carry):
        half = lax.div(t + 1, 2)
        off = n_pair // 2 + jnp.where(lax.rem(t, 2) == 0, half, -half)
        m = lax.rem(mine + off, n_pair)
        best = off_diagonal(qn_v, cn_col, k_v, m * pair, pair)
        j = key_lane + m * pair
        part_v[m] = jnp.maximum(home_v[m], jnp.where(j >= low_n, best, NEG))
        for side in range(2):
            p = 2 * m + side

            @pl.when(p != z)
            def _():
                reduce_copy(p).start()
        return carry

    lax.fori_loop(0, n_pair, next_step, 0)

    both = part_v[mine]
    recv_v[z] = jnp.where(lax.rem(z, 2) == 0, both[:, :rows], both[:, rows:])

    def wait_reduce(s, carry):
        p = lax.rem(z + s, n_z)
        pltpu.make_async_remote_copy(
            src_ref=recv_v.at[p], dst_ref=recv_v.at[p], send_sem=rs_send.at[p], recv_sem=rs_recv.at[p],
            device_id={"qsub": p}, device_id_type=MESH).wait_recv()
        return carry

    lax.fori_loop(1, n_z, wait_reduce, 0)
    own_v[...] = jnp.max(recv_v[...], axis=0) * scale

    def gather_copy(p):
        return pltpu.make_async_remote_copy(
            src_ref=own_v, dst_ref=out_ref.at[z], send_sem=ag_send.at[p], recv_sem=ag_recv.at[z],
            device_id={"qsub": p}, device_id_type=MESH)

    def gather_start(s, carry):
        gather_copy(lax.rem(z + s, n_z)).start()
        return carry

    lax.fori_loop(1, n_z, gather_start, 0)
    keep = pltpu.make_async_copy(own_v, out_ref.at[z], own_sem)
    keep.start()

    def finish(s, carry):
        p = lax.rem(z + s, n_z)
        pltpu.make_async_remote_copy(
            src_ref=own_v, dst_ref=out_ref.at[p], send_sem=ag_send.at[p], recv_sem=ag_recv.at[p],
            device_id={"qsub": p}, device_id_type=MESH).wait()
        reduce_copy(p).wait_send()
        return carry

    lax.fori_loop(1, n_z, finish, 0)
    send_q.wait_send()
    send_c.wait_send()
    keep.wait()


def solution(mesh):
    n_blk, n_z = mesh.shape["blk"], mesh.shape["qsub"]

    def body(queries, key_rows, log_norms, positions):
        rows, head = queries.shape
        n_keys = key_rows.shape[0]
        pair = 2 * rows
        f32 = jnp.float32
        dma = pltpu.SemaphoreType.DMA
        out = pl.pallas_call(
            functools.partial(kernel, n_blk, n_z, head ** -0.5),
            out_shape=jax.ShapeDtypeStruct((n_z, 1, rows), f32),
            in_specs=[pl.BlockSpec(memory_space=pl.ANY)] * 4,
            out_specs=pl.BlockSpec(memory_space=pl.ANY),
            scratch_shapes=[
                pltpu.VMEM((rows, head), jnp.bfloat16),
                pltpu.VMEM((n_keys, head), jnp.bfloat16),
                pltpu.VMEM((rows,), jnp.bfloat16),
                pltpu.VMEM((rows,), jnp.int32),
                pltpu.VMEM((rows, head), jnp.bfloat16),
                pltpu.VMEM((2, rows), f32),
                pltpu.VMEM((2, rows), f32),
                pltpu.VMEM((rows, 128), f32),
                pltpu.VMEM((rows, 128), f32),
                pltpu.VMEM((rows, 128), f32),
                pltpu.VMEM((rows, 128), f32),
                pltpu.VMEM((n_keys // pair, 1, pair), f32),
                pltpu.VMEM((n_keys // pair, 1, pair), f32),
                pltpu.VMEM((n_z, 1, rows), f32),
                pltpu.VMEM((1, rows), f32),
                dma((4,)), dma, dma, dma, dma,
                dma((n_z,)), dma((n_z,)), dma((n_z,)), dma((n_z,)), dma,
            ],
            compiler_params=pltpu.CompilerParams(collective_id=0, has_side_effects=True),
        )(queries, key_rows, log_norms, positions)
        return out.reshape(n_keys)

    in_specs = (P(("blk", "qsub"), None), P("blk", None), P(("blk", "qsub")), P(("blk", "qsub")))
    return jax.shard_map(body, mesh=mesh, in_specs=in_specs, out_specs=P("blk"), check_vma=False)
```

```python
import functools

import jax
import jax.numpy as jnp
from jax import lax
from jax.experimental import pallas as pl
from jax.experimental.pallas import tpu as pltpu
from jax.sharding import PartitionSpec as P

MESH = pl.DeviceIdType.MESH
NEG = -1e30
FAR = 1e30
TILE = 256


def dot_rows(left, right):
    return lax.dot_general(left, right, (((1,), (1,)), ((), ())), preferred_element_type=jnp.float32)


def down(row):
    return jnp.transpose(jnp.broadcast_to(row, (128, row.shape[1])))


def off_diagonal(q_ref, c_ref, k_ref, first, width):
    query = q_ref[...]
    rows = query.shape[0]
    columns = c_ref[...]
    parts = []
    for tile in range(width // TILE):
        keys = k_ref[pl.ds(pl.multiple_of(first + tile * TILE, TILE), TILE), :]
        score = dot_rows(query, keys)
        score = score - jnp.concatenate([columns] * (TILE // 128), axis=1)
        parts.append(jnp.max(score, axis=0, keepdims=True))
    return jnp.concatenate(parts, axis=1)


def kernel(
    n_blk, n_z, near, scale,
    q_hbm, k_hbm, ln_hbm, pos_hbm, out_ref,
    q_v, k_v, ln_v, pos_v, qn_v, cs_v, cn_v, ch_col, cd_col, lo_col, cn_col,
    home_v, part_v, recv_v, full_v,
    in_sem, qs_sem, qr_sem, cs_sem, cr_sem, rs_send, rs_recv, near_send, near_recv, far_send, far_recv, own_sem,
):
    b = lax.axis_index("blk")
    z = lax.axis_index("qsub")
    rows = q_v.shape[0]
    n_keys = k_v.shape[0]
    pair = 2 * rows
    n_pair = n_keys // pair
    before = lax.rem(b + n_blk - 1, n_blk)
    after = lax.rem(b + 1, n_blk)

    barrier = pltpu.get_barrier_semaphore()
    pl.semaphore_signal(barrier, inc=1, device_id={"blk": after}, device_id_type=MESH)

    @pl.when(z == 0)
    def _():
        for p in range(1, n_z):
            pl.semaphore_signal(barrier, inc=1, device_id={"qsub": p}, device_id_type=MESH)

    ins = [
        pltpu.make_async_copy(ln_hbm, ln_v, in_sem.at[0]),
        pltpu.make_async_copy(pos_hbm, pos_v, in_sem.at[1]),
        pltpu.make_async_copy(q_hbm, q_v, in_sem.at[2]),
        pltpu.make_async_copy(k_hbm, k_v, in_sem.at[3]),
    ]
    for copy in ins:
        copy.start()
    ins[0].wait()
    ins[1].wait()

    start = z * rows
    lane = lax.broadcasted_iota(jnp.int32, (1, rows), 1)
    pos = pos_v[...].reshape(1, rows)
    norm = ln_v[...].astype(jnp.float32).reshape(1, rows) * (1.0 / scale)
    first_pos = pos[:, 0:1]
    c_home = jnp.where(pos > lane, norm, FAR)
    c_next = jnp.where(pos > lane + start, norm, FAR)
    low_home = start - first_pos
    low_next = n_keys + start - first_pos
    cs_v[0:1, :] = c_next
    cs_v[1:2, :] = jnp.broadcast_to(low_next.astype(jnp.float32), (1, rows))

    @pl.when(z == 0)
    def _():
        pl.semaphore_wait(barrier, 1)

    @pl.when(z != 0)
    def _():
        pl.semaphore_wait(barrier, 2)

    send_q = pltpu.make_async_remote_copy(
        src_ref=q_hbm, dst_ref=qn_v, send_sem=qs_sem, recv_sem=qr_sem,
        device_id={"blk": before}, device_id_type=MESH)
    send_c = pltpu.make_async_remote_copy(
        src_ref=cs_v, dst_ref=cn_v, send_sem=cs_sem, recv_sem=cr_sem,
        device_id={"blk": before}, device_id_type=MESH)
    send_c.start()
    send_q.start()

    ch_col[...] = down(c_home)
    cd_col[...] = down(norm)
    lo_col[...] = down((lane - pos).astype(jnp.float32))

    home_v[...] = jnp.full(home_v.shape, NEG, jnp.float32)
    ins[2].wait()
    ins[3].wait()
    key_lane = lax.broadcasted_iota(jnp.int32, (1, pair), 1)

    def home_step(m, carry):
        best = off_diagonal(q_v, ch_col, k_v, m * pair, pair)
        j = key_lane + m * pair
        home_v[m] = jnp.where((j >= low_home) & (j < start), best, NEG)
        return carry

    lax.fori_loop(0, lax.div(z, 2) + 1, home_step, 0)

    keys = k_v[pl.ds(pl.multiple_of(start, 128), rows), :]
    score = dot_rows(q_v[...], keys)
    wide = rows // 128
    score = score - jnp.concatenate([cd_col[...]] * wide, axis=1)
    j = lax.broadcasted_iota(jnp.int32, (rows, rows), 1)
    r = lax.broadcasted_iota(jnp.int32, (rows, rows), 0)
    low = jnp.concatenate([lo_col[...]] * wide, axis=1)
    score = jnp.where((j <= r) & (j.astype(jnp.float32) >= low), score, NEG)
    own = jnp.max(score, axis=0, keepdims=True)
    own = jnp.concatenate([own, own], axis=1)
    mine = lax.div(z, 2)
    home_v[mine] = jnp.maximum(home_v[mine], jnp.where(lax.div(key_lane, rows) == lax.rem(z, 2), own, NEG))

    send_c.wait_recv()
    cn = cn_v[...]
    cn_col[...] = down(cn[0:1, :])
    low_n = jnp.where(b < n_blk - 1, cn[1:2, 0:1], jnp.float32(4 * n_keys)).astype(jnp.int32)
    send_q.wait_recv()

    def reduce_copy(m):
        return pltpu.make_async_remote_copy(
            src_ref=part_v.at[m], dst_ref=recv_v.at[m, z], send_sem=rs_send.at[m], recv_sem=rs_recv.at[m],
            device_id={"qsub": 0}, device_id_type=MESH)

    def near_copy(m, p):
        return pltpu.make_async_remote_copy(
            src_ref=full_v.at[m], dst_ref=out_ref.at[m], send_sem=near_send.at[m, p], recv_sem=near_recv.at[m],
            device_id={"qsub": p}, device_id_type=MESH)

    def far_copy(p):
        return pltpu.make_async_remote_copy(
            src_ref=full_v, dst_ref=out_ref, send_sem=far_send.at[p], recv_sem=far_recv,
            device_id={"qsub": p}, device_id_type=MESH)

    def next_step(m, carry):
        best = off_diagonal(qn_v, cn_col, k_v, m * pair, pair)
        j = key_lane + m * pair
        part = jnp.maximum(home_v[m], jnp.where(j >= low_n, best, NEG))

        @pl.when(z == 0)
        def _():
            recv_v[m, 0] = part

        @pl.when(z != 0)
        def _():
            part_v[m] = part
            reduce_copy(m).start()

        return carry

    lax.fori_loop(0, n_pair, next_step, 0)

    @pl.when(z == 0)
    def _():
        def collect(m, carry):
            arrived = recv_v.at[m, pl.ds(1, n_z - 1)]
            pltpu.make_async_copy(arrived, arrived, rs_recv.at[m]).wait()
            full_v[m] = jnp.max(recv_v[m], axis=0) * scale
            for p in range(1, near + 1):
                near_copy(m, p).start()
            return carry

        lax.fori_loop(0, n_pair, collect, 0)
        keep = pltpu.make_async_copy(full_v, out_ref, own_sem)
        keep.start()
        for p in range(near + 1, n_z):
            far_copy(p).start()
        keep.wait()

        def drain(m, carry):
            for p in range(1, near + 1):
                near_copy(m, p).wait_send()
            return carry

        lax.fori_loop(0, n_pair, drain, 0)
        for p in range(near + 1, n_z):
            far_copy(p).wait_send()

    @pl.when(z != 0)
    def _():
        def drain(m, carry):
            reduce_copy(m).wait_send()
            return carry

        lax.fori_loop(0, n_pair, drain, 0)

        @pl.when(z <= near)
        def _():
            def arrive(m, carry):
                near_copy(m, 0).wait_recv()
                return carry

            lax.fori_loop(0, n_pair, arrive, 0)

        @pl.when(z > near)
        def _():
            far_copy(0).wait_recv()

    send_q.wait_send()
    send_c.wait_send()


def solution(mesh):
    n_blk, n_z = mesh.shape["blk"], mesh.shape["qsub"]

    def body(queries, key_rows, log_norms, positions):
        rows, head = queries.shape
        n_keys = key_rows.shape[0]
        pair = 2 * rows
        f32 = jnp.float32
        dma = pltpu.SemaphoreType.DMA
        out = pl.pallas_call(
            functools.partial(kernel, n_blk, n_z, min(4, n_z - 1), head ** -0.5),
            out_shape=jax.ShapeDtypeStruct((n_keys // pair, 1, pair), f32),
            in_specs=[pl.BlockSpec(memory_space=pl.ANY)] * 4,
            out_specs=pl.BlockSpec(memory_space=pl.ANY),
            scratch_shapes=[
                pltpu.VMEM((rows, head), jnp.bfloat16),
                pltpu.VMEM((n_keys, head), jnp.bfloat16),
                pltpu.VMEM((rows,), jnp.bfloat16),
                pltpu.VMEM((rows,), jnp.int32),
                pltpu.VMEM((rows, head), jnp.bfloat16),
                pltpu.VMEM((2, rows), f32),
                pltpu.VMEM((2, rows), f32),
                pltpu.VMEM((rows, 128), f32),
                pltpu.VMEM((rows, 128), f32),
                pltpu.VMEM((rows, 128), f32),
                pltpu.VMEM((rows, 128), f32),
                pltpu.VMEM((n_keys // pair, 1, pair), f32),
                pltpu.VMEM((n_keys // pair, 1, pair), f32),
                pltpu.VMEM((n_keys // pair, n_z, 1, pair), f32),
                pltpu.VMEM((n_keys // pair, 1, pair), f32),
                dma((4,)), dma, dma, dma, dma,
                dma((n_keys // pair,)), dma((n_keys // pair,)),
                dma((n_keys // pair, min(4, n_z - 1) + 1)), dma((n_keys // pair,)),
                dma((n_z,)), dma, dma,
            ],
            compiler_params=pltpu.CompilerParams(collective_id=0, has_side_effects=True),
        )(queries, key_rows, log_norms, positions)
        return out.reshape(n_keys)

    in_specs = (P(("blk", "qsub"), None), P("blk", None), P(("blk", "qsub")), P(("blk", "qsub")))
    return jax.shard_map(body, mesh=mesh, in_specs=in_specs, out_specs=P("blk"), check_vma=False)
```

```python
import functools

import jax
import jax.numpy as jnp
from jax import lax
from jax.experimental import pallas as pl
from jax.experimental.pallas import tpu as pltpu
from jax.sharding import PartitionSpec as P

MESH = pl.DeviceIdType.MESH
NEG = -1e30
FAR = 1e30
TILE = 256
HALVES = 2
PIECES = 2


def plan(n_z):
    if n_z == 16:
        return {0: [1, 2, 3, 4, 15], 3: [5], 4: [7, 6], 15: [8, 9, 10, 11, 12, 13, 14]}, 4
    return {0: list(range(1, n_z))}, 1


def dot_rows(left, right):
    return lax.dot_general(left, right, (((1,), (1,)), ((), ())), preferred_element_type=jnp.float32)


def down(row):
    return jnp.transpose(jnp.broadcast_to(row, (128, row.shape[1])))


def best_of(query, columns, k_ref, first, width):
    parts = []
    for at in range(first, first + width, TILE):
        score = dot_rows(query, k_ref[at : at + TILE, :])
        score = score - jnp.concatenate([columns] * (TILE // 128), axis=1)
        parts.append(jnp.max(score, axis=0, keepdims=True))
    return jnp.concatenate(parts, axis=1)


def kernel(
    n_blk, n_z, scale,
    q_hbm, k_hbm, ln_hbm, pos_hbm, out_ref,
    q_v, k_v, ln_v, pos_v, qn_v, cs_v, cn_v,
    home_v, part_v, recv_v, mid_v, full_v,
    in_sem, qs_sem, qr_sem, cs_sem, cr_sem, rs_send, rs_early, rs_late, ag_send, ag_recv, own_sem,
):
    b = lax.axis_index("blk")
    z = lax.axis_index("qsub")
    sends, n_late = plan(n_z)
    rows = q_v.shape[0]
    n_keys = k_v.shape[0]
    width = n_keys // PIECES
    part_rows = rows // HALVES
    before = lax.rem(b + n_blk - 1, n_blk)
    after = lax.rem(b + 1, n_blk)
    has_before = b > 0
    has_after = b < n_blk - 1
    turn = n_z // 2 - n_late
    slot = lax.rem(z + turn, n_z)
    first_late = n_z - n_late

    barrier = pltpu.get_barrier_semaphore()

    @pl.when(has_after)
    def _():
        pl.semaphore_signal(barrier, inc=1, device_id={"blk": after}, device_id_type=MESH)

    @pl.when(z == 0)
    def _():
        for p in range(1, n_z):
            pl.semaphore_signal(barrier, inc=1, device_id={"qsub": p}, device_id_type=MESH)

    ins = [
        pltpu.make_async_copy(ln_hbm, ln_v, in_sem.at[0]),
        pltpu.make_async_copy(pos_hbm, pos_v, in_sem.at[1]),
        pltpu.make_async_copy(q_hbm, q_v, in_sem.at[2]),
        pltpu.make_async_copy(k_hbm, k_v, in_sem.at[3]),
    ]
    for copy in ins:
        copy.start()
    ins[0].wait()
    ins[1].wait()

    start = z * rows
    lane = lax.broadcasted_iota(jnp.int32, (1, rows), 1)
    pos = pos_v[...].reshape(1, rows)
    norm = ln_v[...].astype(jnp.float32).reshape(1, rows) * (1.0 / scale)
    first_pos = pos[:, 0:1]
    c_home = jnp.where(pos > lane, norm, FAR)
    c_next = jnp.where(pos > lane + start, norm, FAR)
    low_home = start - first_pos
    low_next = n_keys + start - first_pos
    cs_v[0:1, :] = c_next
    cs_v[1:2, :] = jnp.broadcast_to(low_next.astype(jnp.float32), (1, rows))
    ins[2].wait()

    @pl.when(has_before & (z == 0))
    def _():
        pl.semaphore_wait(barrier, 1)

    @pl.when(has_before & (z != 0))
    def _():
        pl.semaphore_wait(barrier, 2)

    send_c = pltpu.make_async_remote_copy(
        src_ref=cs_v, dst_ref=cn_v, send_sem=cs_sem, recv_sem=cr_sem,
        device_id={"blk": before}, device_id_type=MESH)
    send_q = []
    for h in range(HALVES):
        piece = pl.ds(h * part_rows, part_rows)
        send_q.append(pltpu.make_async_remote_copy(
            src_ref=q_v.at[piece], dst_ref=qn_v.at[piece], send_sem=qs_sem.at[h], recv_sem=qr_sem.at[h],
            device_id={"blk": before}, device_id_type=MESH))

    @pl.when(has_before)
    def _():
        send_c.start()
        for copy in send_q:
            copy.start()

    home_columns = down(c_home)
    own_columns = down(norm)
    low_columns = down((lane - pos).astype(jnp.float32))

    ins[3].wait()
    query = q_v[...]
    for g in range(PIECES):
        best = best_of(query, home_columns, k_v, g * width, width)
        j = lax.broadcasted_iota(jnp.int32, (1, width), 1) + g * width
        home_v[0:1, g * width : (g + 1) * width] = jnp.where((j >= low_home) & (j < start), best, NEG)

    here = pl.ds(pl.multiple_of(start, 128), rows)
    score = dot_rows(query, k_v[here, :])
    wide = rows // 128
    score = score - jnp.concatenate([own_columns] * wide, axis=1)
    j = lax.broadcasted_iota(jnp.int32, (rows, rows), 1)
    r = lax.broadcasted_iota(jnp.int32, (rows, rows), 0)
    low = jnp.concatenate([low_columns] * wide, axis=1)
    score = jnp.where((j <= r) & (j.astype(jnp.float32) >= low), score, NEG)
    home_v[0:1, here] = jnp.maximum(home_v[0:1, here], jnp.max(score, axis=0, keepdims=True))

    @pl.when(has_after)
    def _():
        send_c.wait_recv()

    @pl.when(jnp.logical_not(has_after))
    def _():
        cn_v[...] = cs_v[...]
        qn_v[...] = q_v[...]

    cn = cn_v[...]
    next_columns = down(cn[0:1, :])
    low_n = jnp.where(has_after, cn[1:2, 0:1], jnp.float32(4 * n_keys)).astype(jnp.int32)

    def next_best(h, g):
        some = next_columns[h * part_rows : (h + 1) * part_rows, :]
        best = best_of(qn_v[h * part_rows : (h + 1) * part_rows, :], some, k_v, g * width, width)
        j = lax.broadcasted_iota(jnp.int32, (1, width), 1) + g * width
        return jnp.maximum(home_v[0:1, g * width : (g + 1) * width], jnp.where(j >= low_n, best, NEG))

    for h in range(HALVES - 1):
        @pl.when(has_after)
        def _():
            send_q[h].wait_recv()

        for g in range(PIECES):
            home_v[0:1, g * width : (g + 1) * width] = next_best(h, g)

    @pl.when(has_after)
    def _():
        send_q[HALVES - 1].wait_recv()

    def reduce_copy(g, sem):
        return pltpu.make_async_remote_copy(
            src_ref=part_v.at[g], dst_ref=recv_v.at[g, slot], send_sem=rs_send.at[g], recv_sem=sem.at[g],
            device_id={"qsub": 0}, device_id_type=MESH)

    def give(source, target, p, at, g):
        return pltpu.make_async_remote_copy(
            src_ref=source, dst_ref=target, send_sem=ag_send.at[at], recv_sem=ag_recv.at[g],
            device_id={"qsub": p}, device_id_type=MESH)

    @pl.when(z == 0)
    def _():
        for g in range(PIECES):
            recv_v[g, turn] = next_best(HALVES - 1, g)
        for g in range(PIECES):
            arrived = recv_v.at[g, pl.ds(0, first_late - 1)]
            pltpu.make_async_copy(arrived, arrived, rs_early.at[g]).wait()
            mid_v[g] = jnp.max(recv_v[g, 0:first_late], axis=0)
        given, kept = [], []
        for g in range(PIECES):
            arrived = recv_v.at[g, pl.ds(first_late, n_late)]
            pltpu.make_async_copy(arrived, arrived, rs_late.at[g]).wait()
            late = jnp.max(recv_v[g, first_late:n_z], axis=0)
            full_v[g] = jnp.maximum(mid_v[g], late) * scale
            for at, p in enumerate(sends[0]):
                given.append(give(full_v.at[g], out_ref.at[g], p, at * PIECES + g, g))
                given[-1].start()
            keep = pltpu.make_async_copy(full_v.at[g], out_ref.at[g], own_sem.at[g])
            keep.start()
            kept.append(keep)
        for copy in kept:
            copy.wait()
        for copy in given:
            copy.wait_send()

    @pl.when(z != 0)
    def _():
        @pl.when(jnp.logical_not(has_before))
        def _():
            pl.semaphore_wait(barrier, 1)

        late = (z >= n_z // 2) & (z < n_z // 2 + n_late)
        for g in range(PIECES):
            part_v[g] = next_best(HALVES - 1, g)

            @pl.when(late)
            def _():
                reduce_copy(g, rs_late).start()

            @pl.when(jnp.logical_not(late))
            def _():
                reduce_copy(g, rs_early).start()

        direct = z < 0
        for p in sends[0]:
            direct = direct | (z == p)

        @pl.when(direct)
        def _():
            for g in range(PIECES):
                give(out_ref.at[g], out_ref.at[g], 0, 0, g).wait_recv()

        @pl.when(jnp.logical_not(direct))
        def _():
            give(out_ref, out_ref, 0, 0, 0).wait_recv()

        for source, targets in sends.items():
            if source == 0:
                continue

            @pl.when(z == source)
            def _():
                given = []
                for at, p in enumerate(targets):
                    given.append(give(out_ref, out_ref, p, at, 0))
                    given[-1].start()
                for copy in given:
                    copy.wait_send()

        for g in range(PIECES):
            reduce_copy(g, rs_early).wait_send()

    @pl.when(has_before)
    def _():
        send_c.wait_send()
        for copy in send_q:
            copy.wait_send()


def solution(mesh):
    n_blk, n_z = mesh.shape["blk"], mesh.shape["qsub"]

    def body(queries, key_rows, log_norms, positions):
        rows, head = queries.shape
        n_keys = key_rows.shape[0]
        width = n_keys // PIECES
        f32 = jnp.float32
        dma = pltpu.SemaphoreType.DMA
        operands = [
            pltpu.with_memory_space_constraint(x, pltpu.HBM) for x in (queries, key_rows, log_norms, positions)
        ]
        out = pl.pallas_call(
            functools.partial(kernel, n_blk, n_z, head ** -0.5),
            out_shape=pltpu.VMEM((PIECES, 1, width), f32),
            in_specs=[pl.BlockSpec(memory_space=pl.ANY)] * 4,
            out_specs=pl.BlockSpec(memory_space=pl.ANY),
            scratch_shapes=[
                pltpu.VMEM((rows, head), jnp.bfloat16),
                pltpu.VMEM((n_keys, head), jnp.bfloat16),
                pltpu.VMEM((rows,), jnp.bfloat16),
                pltpu.VMEM((rows,), jnp.int32),
                pltpu.VMEM((rows, head), jnp.bfloat16),
                pltpu.VMEM((2, rows), f32),
                pltpu.VMEM((2, rows), f32),
                pltpu.VMEM((1, n_keys), f32),
                pltpu.VMEM((PIECES, 1, width), f32),
                pltpu.VMEM((PIECES, n_z, 1, width), f32),
                pltpu.VMEM((PIECES, 1, width), f32),
                pltpu.VMEM((PIECES, 1, width), f32),
                dma((4,)), dma((HALVES,)), dma((HALVES,)), dma, dma,
                dma((PIECES,)), dma((PIECES,)), dma((PIECES,)), dma((PIECES * n_z,)), dma((PIECES,)), dma((PIECES,)),
            ],
            compiler_params=pltpu.CompilerParams(
                collective_id=0, has_side_effects=True, vmem_limit_bytes=16 * 1024 * 1024),
        )(*operands)
        return out.reshape(n_keys)

    in_specs = (P(("blk", "qsub"), None), P("blk", None), P(("blk", "qsub")), P(("blk", "qsub")))
    return jax.shard_map(body, mesh=mesh, in_specs=in_specs, out_specs=P("blk"), check_vma=False)
```

```python
import functools

import jax
import jax.numpy as jnp
from jax import lax
from jax.experimental import pallas as pl
from jax.experimental.pallas import tpu as pltpu
from jax.sharding import PartitionSpec as P

MESH = pl.DeviceIdType.MESH
NEG = -1e30
FAR = 1e30
TILE = 256
HALVES = 2
PIECES = 2
STEPS = 65000.0


def plan(n_z):
    if n_z == 16:
        return {0: [1, 4, 2, 5, 3, 15], 4: [6], 5: [7], 15: [8, 9, 10, 11, 12, 13, 14]}, 4
    return {0: list(range(1, n_z))}, 1


def dot_rows(left, right):
    return lax.dot_general(left, right, (((1,), (1,)), ((), ())), preferred_element_type=jnp.float32)


def down(row):
    return jnp.transpose(jnp.broadcast_to(row, (128, row.shape[1])))


def fold(groups):
    number = len(groups)
    groups = groups + [groups[-1]] * (8 - number)
    row = lax.broadcasted_iota(jnp.int32, (8, 128), 0)
    for by in (4, 2, 1):
        upper = (row & by) == 0
        groups = [
            jnp.where(
                upper,
                jnp.maximum(groups[i], pltpu.roll(groups[i], 8 - by, 0)),
                jnp.maximum(groups[i + by], pltpu.roll(groups[i + by], by, 0)),
            )
            for i in range(by)
        ]
    return groups[0] if number == 8 else groups[0][:number]


def dense(groups):
    return jnp.concatenate([fold(groups[i : i + 8]) for i in range(0, len(groups), 8)], axis=0)


def eighths(score):
    rows, width = score.shape
    best = jnp.max(score.reshape(rows // 8, 8, width), axis=0)
    return [best[:, i : i + 128] for i in range(0, width, 128)]


def best_of(query, columns, k_ref, first, width):
    groups = []
    for at in range(first, first + width, TILE):
        score = dot_rows(query, k_ref[at : at + TILE, :])
        score = score - jnp.concatenate([columns] * (TILE // 128), axis=1)
        groups += eighths(score)
    return dense(groups)


def key_index(g, lines):
    line = lax.broadcasted_iota(jnp.int32, (lines, 128), 0) + g * lines
    return line * 128 + lax.broadcasted_iota(jnp.int32, (lines, 128), 1)


def encode(best):
    low = jnp.min(best, axis=0, keepdims=True)
    span = jnp.maximum(jnp.max(best, axis=0, keepdims=True) - low, 1e-6)
    steps = jnp.round((best - low) * (STEPS / span)) - STEPS / 2
    return steps.astype(jnp.int32).astype(jnp.int16), jnp.concatenate([low, span * (1.0 / STEPS)], axis=0)


def decode(code, bounds):
    steps = code.astype(jnp.int32).astype(jnp.float32) + STEPS / 2
    return steps * bounds[1:2, :] + bounds[0:1, :]


def kernel(
    n_blk, n_z, scale,
    q_hbm, k_hbm, ln_hbm, pos_hbm, out_ref,
    q_v, k_v, ln_v, pos_v, qn_v, cs_v, cn_v,
    home_v, part_v, recv_v, mid_v, code_v, bound_v,
    in_sem, qs_sem, qr_sem, cs_sem, cr_sem, rs_send, rs_early, rs_late, ag_send, ag_recv,
):
    b = lax.axis_index("blk")
    z = lax.axis_index("qsub")
    sends, n_late = plan(n_z)
    rows = q_v.shape[0]
    n_keys = k_v.shape[0]
    width = n_keys // PIECES
    lines = width // 128
    part_rows = rows // HALVES
    before = lax.rem(b + n_blk - 1, n_blk)
    after = lax.rem(b + 1, n_blk)
    has_before = b > 0
    has_after = b < n_blk - 1
    turn = n_z // 2 - n_late
    slot = lax.rem(z + turn, n_z)
    first_late = n_z - n_late

    barrier = pltpu.get_barrier_semaphore()

    @pl.when(has_after)
    def _():
        pl.semaphore_signal(barrier, inc=1, device_id={"blk": after}, device_id_type=MESH)

    @pl.when(z == 0)
    def _():
        for p in range(1, n_z):
            pl.semaphore_signal(barrier, inc=1, device_id={"qsub": p}, device_id_type=MESH)

    ins = [
        pltpu.make_async_copy(ln_hbm, ln_v, in_sem.at[0]),
        pltpu.make_async_copy(pos_hbm, pos_v, in_sem.at[1]),
        pltpu.make_async_copy(q_hbm, q_v, in_sem.at[2]),
        pltpu.make_async_copy(k_hbm, k_v, in_sem.at[3]),
    ]
    for copy in ins:
        copy.start()
    ins[0].wait()
    ins[1].wait()

    start = z * rows
    lane = lax.broadcasted_iota(jnp.int32, (1, rows), 1)
    pos = pos_v[...].reshape(1, rows)
    norm = ln_v[...].astype(jnp.float32).reshape(1, rows) * (1.0 / scale)
    first_pos = pos[:, 0:1]
    c_home = jnp.where(pos > lane, norm, FAR)
    c_next = jnp.where(pos > lane + start, norm, FAR)
    low_home = start - first_pos
    low_next = n_keys + start - first_pos
    cs_v[0:1, :] = c_next
    cs_v[1:2, :] = jnp.broadcast_to(low_next.astype(jnp.float32), (1, rows))
    ins[2].wait()

    @pl.when(has_before & (z == 0))
    def _():
        pl.semaphore_wait(barrier, 1)

    @pl.when(has_before & (z != 0))
    def _():
        pl.semaphore_wait(barrier, 2)

    send_c = pltpu.make_async_remote_copy(
        src_ref=cs_v, dst_ref=cn_v, send_sem=cs_sem, recv_sem=cr_sem,
        device_id={"blk": before}, device_id_type=MESH)
    send_q = []
    for h in range(HALVES):
        piece = pl.ds(h * part_rows, part_rows)
        send_q.append(pltpu.make_async_remote_copy(
            src_ref=q_v.at[piece], dst_ref=qn_v.at[piece], send_sem=qs_sem.at[h], recv_sem=qr_sem.at[h],
            device_id={"blk": before}, device_id_type=MESH))

    @pl.when(has_before)
    def _():
        send_c.start()
        for copy in send_q:
            copy.start()

    home_columns = down(c_home)
    own_columns = down(norm)
    low_columns = down((lane - pos).astype(jnp.float32))

    ins[3].wait()
    query = q_v[...]
    for g in range(PIECES):
        best = best_of(query, home_columns, k_v, g * width, width)
        j = key_index(g, lines)
        home_v[g * lines : (g + 1) * lines, :] = jnp.where((j >= low_home) & (j < start), best, NEG)

    here = pl.ds(pl.multiple_of(start, 128), rows)
    score = dot_rows(query, k_v[here, :])
    wide = rows // 128
    score = score - jnp.concatenate([own_columns] * wide, axis=1)
    j = lax.broadcasted_iota(jnp.int32, (rows, rows), 1)
    r = lax.broadcasted_iota(jnp.int32, (rows, rows), 0)
    low = jnp.concatenate([low_columns] * wide, axis=1)
    score = jnp.where((j <= r) & (j.astype(jnp.float32) >= low), score, NEG)
    own = dense(eighths(score))
    mine = pl.ds(z * wide, wide)
    home_v[mine, :] = jnp.maximum(home_v[mine, :], own)

    @pl.when(has_after)
    def _():
        send_c.wait_recv()

    @pl.when(jnp.logical_not(has_after))
    def _():
        cn_v[...] = cs_v[...]
        qn_v[...] = q_v[...]

    cn = cn_v[...]
    next_columns = down(cn[0:1, :])
    low_n = jnp.where(has_after, cn[1:2, 0:1], jnp.float32(4 * n_keys)).astype(jnp.int32)

    def next_best(h, g):
        some = next_columns[h * part_rows : (h + 1) * part_rows, :]
        best = best_of(qn_v[h * part_rows : (h + 1) * part_rows, :], some, k_v, g * width, width)
        return jnp.maximum(
            home_v[g * lines : (g + 1) * lines, :], jnp.where(key_index(g, lines) >= low_n, best, NEG))

    for h in range(HALVES - 1):
        @pl.when(has_after)
        def _():
            send_q[h].wait_recv()

        for g in range(PIECES):
            home_v[g * lines : (g + 1) * lines, :] = next_best(h, g)

    @pl.when(has_after)
    def _():
        send_q[HALVES - 1].wait_recv()

    def reduce_copy(g, sem):
        return pltpu.make_async_remote_copy(
            src_ref=part_v.at[g], dst_ref=recv_v.at[g, slot], send_sem=rs_send.at[g], recv_sem=sem.at[g],
            device_id={"qsub": 0}, device_id_type=MESH)

    def give(p, at):
        return [
            pltpu.make_async_remote_copy(
                src_ref=ref, dst_ref=ref, send_sem=ag_send.at[2 * at + i], recv_sem=ag_recv.at[i],
                device_id={"qsub": p}, device_id_type=MESH)
            for i, ref in enumerate((bound_v, code_v))
        ]

    def pass_on(source, done):
        for at, p in enumerate(sends[source]):
            for copy in give(p, at):
                if done:
                    copy.wait_send()
                else:
                    copy.start()

    @pl.when(z == 0)
    def _():
        for g in range(PIECES):
            recv_v[g, turn] = next_best(HALVES - 1, g)
        for g in range(PIECES):
            arrived = recv_v.at[g, pl.ds(0, first_late - 1)]
            pltpu.make_async_copy(arrived, arrived, rs_early.at[g]).wait()
            mid_v[g] = jnp.max(recv_v[g, 0:first_late], axis=0)
        full = []
        for g in range(PIECES):
            arrived = recv_v.at[g, pl.ds(first_late, n_late)]
            pltpu.make_async_copy(arrived, arrived, rs_late.at[g]).wait()
            full.append(jnp.maximum(mid_v[g], jnp.max(recv_v[g, first_late:n_z], axis=0)) * scale)
        code, bounds = encode(jnp.concatenate(full, axis=0))
        code_v[...] = code
        bound_v[...] = bounds

    @pl.when(z != 0)
    def _():
        @pl.when(jnp.logical_not(has_before))
        def _():
            pl.semaphore_wait(barrier, 1)

        late = (z >= n_z // 2) & (z < n_z // 2 + n_late)
        for g in range(PIECES):
            part_v[g] = next_best(HALVES - 1, g)

            @pl.when(late)
            def _():
                reduce_copy(g, rs_late).start()

            @pl.when(jnp.logical_not(late))
            def _():
                reduce_copy(g, rs_early).start()

        for copy in give(0, 0):
            copy.wait_recv()

    for source in sends:
        pl.when(z == source)(functools.partial(pass_on, source, False))

    out_ref[...] = decode(code_v[...], bound_v[...])

    for source in sends:
        pl.when(z == source)(functools.partial(pass_on, source, True))

    @pl.when(z != 0)
    def _():
        for g in range(PIECES):
            reduce_copy(g, rs_early).wait_send()

    @pl.when(has_before)
    def _():
        send_c.wait_send()
        for copy in send_q:
            copy.wait_send()


def solution(mesh):
    n_blk, n_z = mesh.shape["blk"], mesh.shape["qsub"]

    def body(queries, key_rows, log_norms, positions):
        rows, head = queries.shape
        n_keys = key_rows.shape[0]
        lines = n_keys // PIECES // 128
        f32 = jnp.float32
        dma = pltpu.SemaphoreType.DMA
        operands = [
            pltpu.with_memory_space_constraint(x, pltpu.HBM) for x in (queries, key_rows, log_norms, positions)
        ]
        out = pl.pallas_call(
            functools.partial(kernel, n_blk, n_z, head ** -0.5),
            out_shape=pltpu.VMEM((n_keys // 128, 128), f32),
            in_specs=[pl.BlockSpec(memory_space=pl.ANY)] * 4,
            out_specs=pl.BlockSpec(memory_space=pltpu.VMEM),
            scratch_shapes=[
                pltpu.VMEM((rows, head), jnp.bfloat16),
                pltpu.VMEM((n_keys, head), jnp.bfloat16),
                pltpu.VMEM((rows,), jnp.bfloat16),
                pltpu.VMEM((rows,), jnp.int32),
                pltpu.VMEM((rows, head), jnp.bfloat16),
                pltpu.VMEM((2, rows), f32),
                pltpu.VMEM((2, rows), f32),
                pltpu.VMEM((n_keys // 128, 128), f32),
                pltpu.VMEM((PIECES, lines, 128), f32),
                pltpu.VMEM((PIECES, n_z, lines, 128), f32),
                pltpu.VMEM((PIECES, lines, 128), f32),
                pltpu.VMEM((n_keys // 128, 128), jnp.int16),
                pltpu.VMEM((2, 128), f32),
                dma((4,)), dma((HALVES,)), dma((HALVES,)), dma, dma,
                dma((PIECES,)), dma((PIECES,)), dma((PIECES,)), dma((2 * n_z,)), dma((2,)),
            ],
            compiler_params=pltpu.CompilerParams(
                collective_id=0, has_side_effects=True, vmem_limit_bytes=16 * 1024 * 1024),
        )(*operands)
        return out.reshape(n_keys)

    in_specs = (P(("blk", "qsub"), None), P("blk", None), P(("blk", "qsub")), P(("blk", "qsub")))
    return jax.shard_map(body, mesh=mesh, in_specs=in_specs, out_specs=P("blk"), check_vma=False)
```

```python
import functools

import jax
import jax.numpy as jnp
from jax import lax
from jax.experimental import pallas as pl
from jax.experimental.pallas import tpu as pltpu
from jax.sharding import PartitionSpec as P

MESH = pl.DeviceIdType.MESH
NEG = -1e30
FAR = 1e30
TILE = 256
HALVES = 2
PIECES = 3
ROW = 8
STEPS = 65000.0


def plan(n_z):
    if n_z == 16:
        return {0: [1, 4, 2, 15, 3], 4: [5, 6, 7], 15: [8, 9, 10, 11, 12, 13, 14]}, 4
    return {0: list(range(1, n_z))}, 1


def dot_rows(left, right):
    return lax.dot_general(left, right, (((1,), (1,)), ((), ())), preferred_element_type=jnp.float32)


def down(row):
    return jnp.transpose(jnp.broadcast_to(row, (128, row.shape[1])))


def fold(groups):
    number = len(groups)
    groups = groups + [groups[-1]] * (8 - number)
    row = lax.broadcasted_iota(jnp.int32, (8, 128), 0)
    for by in (4, 2, 1):
        upper = (row & by) == 0
        groups = [
            jnp.where(
                upper,
                jnp.maximum(groups[i], pltpu.roll(groups[i], 8 - by, 0)),
                jnp.maximum(groups[i + by], pltpu.roll(groups[i + by], by, 0)),
            )
            for i in range(by)
        ]
    return groups[0] if number == 8 else groups[0][:number]


def dense(groups):
    return jnp.concatenate([fold(groups[i : i + 8]) for i in range(0, len(groups), 8)], axis=0)


def eighths(score):
    rows, width = score.shape
    best = jnp.max(score.reshape(rows // 8, 8, width), axis=0)
    return [best[:, i : i + 128] for i in range(0, width, 128)]


def best_of(query, columns, k_ref, first, width):
    groups = []
    for at in range(first, first + width, TILE):
        score = dot_rows(query, k_ref[at : at + TILE, :])
        score = score - jnp.concatenate([columns] * (TILE // 128), axis=1)
        groups += eighths(score)
    return dense(groups)


def key_index(g, lines):
    line = lax.broadcasted_iota(jnp.int32, (lines, 128), 0) + g * lines
    return line * 128 + lax.broadcasted_iota(jnp.int32, (lines, 128), 1)


def encode(best):
    low = jnp.min(best, axis=0, keepdims=True)
    span = jnp.maximum(jnp.max(best, axis=0, keepdims=True) - low, 1e-6)
    steps = jnp.round((best - low) * (STEPS / span)) - STEPS / 2
    return steps.astype(jnp.int32).astype(jnp.int16), jnp.concatenate([low, span * (1.0 / STEPS)], axis=0)


def decode(code, bounds):
    steps = code.astype(jnp.int32).astype(jnp.float32) + STEPS / 2
    return steps * bounds[1:2, :] + bounds[0:1, :]


def kernel(
    n_blk, n_z, scale,
    q_hbm, k_hbm, ln_hbm, pos_hbm, code_v, bound_v,
    q_v, k_v, ln_v, pos_v, qn_v, cs_v, cn_v,
    home_v, part_v, recv_v, mid_v,
    in_sem, qs_sem, qr_sem, cs_sem, cr_sem, rs_send, rs_early, rs_late, ag_send, ag_recv,
):
    b = lax.axis_index("blk")
    z = lax.axis_index("qsub")
    sends, n_late = plan(n_z)
    rows = q_v.shape[0]
    n_keys = k_v.shape[0]
    width = n_keys // PIECES
    lines = width // 128
    part_rows = rows // HALVES
    before = lax.rem(b + n_blk - 1, n_blk)
    after = lax.rem(b + 1, n_blk)
    has_before = b > 0
    has_after = b < n_blk - 1
    turn = n_z // 2 - n_late
    slot = lax.rem(z + turn, n_z)
    first_late = n_z - n_late

    barrier = pltpu.get_barrier_semaphore()

    @pl.when(has_after)
    def _():
        pl.semaphore_signal(barrier, inc=1, device_id={"blk": after}, device_id_type=MESH)

    @pl.when(z == 0)
    def _():
        for p in range(1, n_z):
            pl.semaphore_signal(barrier, inc=1, device_id={"qsub": p}, device_id_type=MESH)

    ins = [
        pltpu.make_async_copy(ln_hbm, ln_v, in_sem.at[0]),
        pltpu.make_async_copy(pos_hbm, pos_v, in_sem.at[1]),
        pltpu.make_async_copy(q_hbm, q_v, in_sem.at[2]),
        pltpu.make_async_copy(k_hbm, k_v, in_sem.at[3]),
    ]
    for copy in ins:
        copy.start()
    ins[0].wait()
    ins[1].wait()

    start = z * rows
    lane = lax.broadcasted_iota(jnp.int32, (1, rows), 1)
    pos = pos_v[...].reshape(1, rows)
    norm = ln_v[...].astype(jnp.float32).reshape(1, rows) * (1.0 / scale)
    first_pos = pos[:, 0:1]
    c_home = jnp.where(pos > lane, norm, FAR)
    c_next = jnp.where(pos > lane + start, norm, FAR)
    low_home = start - first_pos
    low_next = n_keys + start - first_pos
    cs_v[0:1, :] = c_next
    cs_v[1:2, :] = jnp.broadcast_to(low_next.astype(jnp.float32), (1, rows))
    ins[2].wait()

    send_c = pltpu.make_async_remote_copy(
        src_ref=cs_v, dst_ref=cn_v, send_sem=cs_sem, recv_sem=cr_sem,
        device_id={"blk": before}, device_id_type=MESH)
    send_q = []
    for h in range(HALVES):
        piece = pl.ds(h * part_rows, part_rows)
        send_q.append(pltpu.make_async_remote_copy(
            src_ref=q_v.at[piece], dst_ref=qn_v.at[piece], send_sem=qs_sem.at[h], recv_sem=qr_sem.at[h],
            device_id={"blk": before}, device_id_type=MESH))

    def send_queries():
        @pl.when(z == 0)
        def _():
            pl.semaphore_wait(barrier, 1)

        @pl.when(z != 0)
        def _():
            pl.semaphore_wait(barrier, 2)

        send_c.start()
        for copy in send_q:
            copy.start()

    far = lax.rem(b, ROW) == 0
    pl.when(has_before & jnp.logical_not(far))(send_queries)

    home_columns = down(c_home)
    own_columns = down(norm)
    low_columns = down((lane - pos).astype(jnp.float32))

    ins[3].wait()
    query = q_v[...]
    for g in range(PIECES):
        best = best_of(query, home_columns, k_v, g * width, width)
        j = key_index(g, lines)
        home_v[g * lines : (g + 1) * lines, :] = jnp.where((j >= low_home) & (j < start), best, NEG)
        if g == 0:
            pl.when(has_before & far)(send_queries)

    here = pl.ds(pl.multiple_of(start, 128), rows)
    score = dot_rows(query, k_v[here, :])
    wide = rows // 128
    score = score - jnp.concatenate([own_columns] * wide, axis=1)
    j = lax.broadcasted_iota(jnp.int32, (rows, rows), 1)
    r = lax.broadcasted_iota(jnp.int32, (rows, rows), 0)
    low = jnp.concatenate([low_columns] * wide, axis=1)
    score = jnp.where((j <= r) & (j.astype(jnp.float32) >= low), score, NEG)
    own = dense(eighths(score))
    mine = pl.ds(z * wide, wide)
    home_v[mine, :] = jnp.maximum(home_v[mine, :], own)

    @pl.when(has_after)
    def _():
        send_c.wait_recv()

    @pl.when(jnp.logical_not(has_after))
    def _():
        cn_v[...] = cs_v[...]
        qn_v[...] = q_v[...]

    cn = cn_v[...]
    next_columns = down(cn[0:1, :])
    low_n = jnp.where(has_after, cn[1:2, 0:1], jnp.float32(4 * n_keys)).astype(jnp.int32)

    def next_best(h, g):
        some = next_columns[h * part_rows : (h + 1) * part_rows, :]
        best = best_of(qn_v[h * part_rows : (h + 1) * part_rows, :], some, k_v, g * width, width)
        return jnp.maximum(
            home_v[g * lines : (g + 1) * lines, :], jnp.where(key_index(g, lines) >= low_n, best, NEG))

    for h in range(HALVES - 1):
        @pl.when(has_after)
        def _():
            send_q[h].wait_recv()

        for g in range(PIECES):
            home_v[g * lines : (g + 1) * lines, :] = next_best(h, g)

    @pl.when(has_after)
    def _():
        send_q[HALVES - 1].wait_recv()

    def reduce_copy(g, sem):
        return pltpu.make_async_remote_copy(
            src_ref=part_v.at[g], dst_ref=recv_v.at[g, slot], send_sem=rs_send.at[g], recv_sem=sem.at[g],
            device_id={"qsub": 0}, device_id_type=MESH)

    def give(p, at):
        return [
            pltpu.make_async_remote_copy(
                src_ref=ref, dst_ref=ref, send_sem=ag_send.at[2 * at + i], recv_sem=ag_recv.at[i],
                device_id={"qsub": p}, device_id_type=MESH)
            for i, ref in enumerate((bound_v, code_v))
        ]

    def pass_on(source, done):
        for at, p in enumerate(sends[source]):
            for copy in give(p, at):
                if done:
                    copy.wait_send()
                else:
                    copy.start()

    @pl.when(z == 0)
    def _():
        for g in range(PIECES):
            recv_v[g, turn] = next_best(HALVES - 1, g)
        for g in range(PIECES):
            arrived = recv_v.at[g, pl.ds(0, first_late - 1)]
            pltpu.make_async_copy(arrived, arrived, rs_early.at[g]).wait()
            mid_v[g] = jnp.max(recv_v[g, 0:first_late], axis=0)
        full = []
        for g in range(PIECES):
            arrived = recv_v.at[g, pl.ds(first_late, n_late)]
            pltpu.make_async_copy(arrived, arrived, rs_late.at[g]).wait()
            full.append(jnp.maximum(mid_v[g], jnp.max(recv_v[g, first_late:n_z], axis=0)) * scale)
        code, bounds = encode(jnp.concatenate(full, axis=0))
        code_v[...] = code
        bound_v[...] = bounds

    @pl.when(z != 0)
    def _():
        @pl.when(jnp.logical_not(has_before))
        def _():
            pl.semaphore_wait(barrier, 1)

        late = (z >= n_z // 2) & (z < n_z // 2 + n_late)
        for g in range(PIECES):
            part_v[g] = next_best(HALVES - 1, g)

            @pl.when(late)
            def _():
                reduce_copy(g, rs_late).start()

            @pl.when(jnp.logical_not(late))
            def _():
                reduce_copy(g, rs_early).start()

        for copy in give(0, 0):
            copy.wait_recv()

    for source in sends:
        pl.when(z == source)(functools.partial(pass_on, source, False))

    for source in sends:
        pl.when(z == source)(functools.partial(pass_on, source, True))

    @pl.when(z != 0)
    def _():
        for g in range(PIECES):
            reduce_copy(g, rs_early).wait_send()

    @pl.when(has_before)
    def _():
        send_c.wait_send()
        for copy in send_q:
            copy.wait_send()


def solution(mesh):
    n_blk, n_z = mesh.shape["blk"], mesh.shape["qsub"]

    def body(queries, key_rows, log_norms, positions):
        rows, head = queries.shape
        n_keys = key_rows.shape[0]
        lines = n_keys // PIECES // 128
        f32 = jnp.float32
        dma = pltpu.SemaphoreType.DMA
        operands = [
            pltpu.with_memory_space_constraint(x, pltpu.HBM) for x in (queries, key_rows, log_norms, positions)
        ]
        code, bounds = pl.pallas_call(
            functools.partial(kernel, n_blk, n_z, head ** -0.5),
            out_shape=(pltpu.VMEM((n_keys // 128, 128), jnp.int16), pltpu.VMEM((2, 128), f32)),
            in_specs=[pl.BlockSpec(memory_space=pl.ANY)] * 4,
            out_specs=[pl.BlockSpec(memory_space=pltpu.VMEM)] * 2,
            scratch_shapes=[
                pltpu.VMEM((rows, head), jnp.bfloat16),
                pltpu.VMEM((n_keys, head), jnp.bfloat16),
                pltpu.VMEM((rows,), jnp.bfloat16),
                pltpu.VMEM((rows,), jnp.int32),
                pltpu.VMEM((rows, head), jnp.bfloat16),
                pltpu.VMEM((2, rows), f32),
                pltpu.VMEM((2, rows), f32),
                pltpu.VMEM((n_keys // 128, 128), f32),
                pltpu.VMEM((PIECES, lines, 128), f32),
                pltpu.VMEM((PIECES, n_z, lines, 128), f32),
                pltpu.VMEM((PIECES, lines, 128), f32),
                dma((4,)), dma((HALVES,)), dma((HALVES,)), dma, dma,
                dma((PIECES,)), dma((PIECES,)), dma((PIECES,)), dma((2 * n_z,)), dma((2,)),
            ],
            compiler_params=pltpu.CompilerParams(
                collective_id=0, has_side_effects=True, vmem_limit_bytes=16 * 1024 * 1024),
        )(*operands)
        return decode(code, bounds).reshape(n_keys)

    in_specs = (P(("blk", "qsub"), None), P("blk", None), P(("blk", "qsub")), P(("blk", "qsub")))
    return jax.shard_map(body, mesh=mesh, in_specs=in_specs, out_specs=P("blk"), check_vma=False)
```

```python
import functools

import jax
import jax.numpy as jnp
from jax import lax
from jax.experimental import pallas as pl
from jax.experimental.pallas import tpu as pltpu
from jax.sharding import PartitionSpec as P

MESH = pl.DeviceIdType.MESH
NEG = -1e30
FAR = 1e30
TILE = 256
HALVES = 2
PIECES = (2, 1)
HOME = 3
ROW = 8
STEPS = 65000.0


def plan(n_z):
    if n_z == 16:
        return {0: [1, 4, 2, 15, 3], 4: [5, 6, 7], 15: [8, 9, 10, 11, 12, 13, 14]}, 4
    return {0: list(range(1, n_z))}, 1


def dot_rows(left, right):
    return lax.dot_general(left, right, (((1,), (1,)), ((), ())), preferred_element_type=jnp.float32)


def down(row):
    return jnp.transpose(jnp.broadcast_to(row, (128, row.shape[1])))


def fold(groups):
    number = len(groups)
    groups = groups + [groups[-1]] * (8 - number)
    row = lax.broadcasted_iota(jnp.int32, (8, 128), 0)
    for by in (4, 2, 1):
        upper = (row & by) == 0
        groups = [
            jnp.where(
                upper,
                jnp.maximum(groups[i], pltpu.roll(groups[i], 8 - by, 0)),
                jnp.maximum(groups[i + by], pltpu.roll(groups[i + by], by, 0)),
            )
            for i in range(by)
        ]
    return groups[0] if number == 8 else groups[0][:number]


def dense(groups):
    return jnp.concatenate([fold(groups[i : i + 8]) for i in range(0, len(groups), 8)], axis=0)


def eighths(score):
    rows, width = score.shape
    best = jnp.max(score.reshape(rows // 8, 8, width), axis=0)
    return [best[:, i : i + 128] for i in range(0, width, 128)]


def best_of(query, columns, k_ref, first, width):
    groups = []
    for at in range(first, first + width, TILE):
        score = dot_rows(query, k_ref[at : at + TILE, :])
        score = score - jnp.concatenate([columns] * (TILE // 128), axis=1)
        groups += eighths(score)
    return dense(groups)


def key_index(first, lines):
    line = lax.broadcasted_iota(jnp.int32, (lines, 128), 0) + first
    return line * 128 + lax.broadcasted_iota(jnp.int32, (lines, 128), 1)


def cut(n_keys):
    unit = n_keys // 128 // sum(PIECES)
    return [(sum(PIECES[:g]) * unit, PIECES[g] * unit) for g in range(len(PIECES))]


def encode(best):
    low = jnp.min(best, axis=0, keepdims=True)
    span = jnp.maximum(jnp.max(best, axis=0, keepdims=True) - low, 1e-6)
    steps = jnp.round((best - low) * (STEPS / span)) - STEPS / 2
    return steps.astype(jnp.int32).astype(jnp.int16), jnp.concatenate([low, span * (1.0 / STEPS)], axis=0)


def decode(code, bounds):
    steps = code.astype(jnp.int32).astype(jnp.float32) + STEPS / 2
    return steps * bounds[1:2, :] + bounds[0:1, :]


def kernel(
    n_blk, n_z, scale,
    q_hbm, k_hbm, ln_hbm, pos_hbm, code_v, bound_v,
    q_v, k_v, ln_v, pos_v, qn_v, cs_v, cn_v,
    home_v, part_0, part_1, recv_0, recv_1, mid_0, mid_1,
    in_sem, qs_sem, qr_sem, cs_sem, cr_sem, rs_send, rs_early, rs_late, ag_send, ag_recv,
):
    b = lax.axis_index("blk")
    z = lax.axis_index("qsub")
    sends, n_late = plan(n_z)
    rows = q_v.shape[0]
    n_keys = k_v.shape[0]
    cuts = list(enumerate(cut(n_keys)))
    part_v, recv_v, mid_v = (part_0, part_1), (recv_0, recv_1), (mid_0, mid_1)
    home_lines = n_keys // 128 // HOME
    part_rows = rows // HALVES
    before = lax.rem(b + n_blk - 1, n_blk)
    after = lax.rem(b + 1, n_blk)
    has_before = b > 0
    has_after = b < n_blk - 1
    turn = n_z // 2 - n_late
    slot = lax.rem(z + turn, n_z)
    first_late = n_z - n_late

    barrier = pltpu.get_barrier_semaphore()

    @pl.when(has_after)
    def _():
        pl.semaphore_signal(barrier, inc=1, device_id={"blk": after}, device_id_type=MESH)

    @pl.when(z == 0)
    def _():
        for p in range(1, n_z):
            pl.semaphore_signal(barrier, inc=1, device_id={"qsub": p}, device_id_type=MESH)

    ins = [
        pltpu.make_async_copy(ln_hbm, ln_v, in_sem.at[0]),
        pltpu.make_async_copy(pos_hbm, pos_v, in_sem.at[1]),
        pltpu.make_async_copy(q_hbm, q_v, in_sem.at[2]),
        pltpu.make_async_copy(k_hbm, k_v, in_sem.at[3]),
    ]
    for copy in ins:
        copy.start()
    ins[0].wait()
    ins[1].wait()

    start = z * rows
    lane = lax.broadcasted_iota(jnp.int32, (1, rows), 1)
    pos = pos_v[...].reshape(1, rows)
    norm = ln_v[...].astype(jnp.float32).reshape(1, rows) * (1.0 / scale)
    first_pos = pos[:, 0:1]
    c_home = jnp.where(pos > lane, norm, FAR)
    c_next = jnp.where(pos > lane + start, norm, FAR)
    low_home = start - first_pos
    low_next = n_keys + start - first_pos
    cs_v[0:1, :] = c_next
    cs_v[1:2, :] = jnp.broadcast_to(low_next.astype(jnp.float32), (1, rows))
    ins[2].wait()

    send_c = pltpu.make_async_remote_copy(
        src_ref=cs_v, dst_ref=cn_v, send_sem=cs_sem, recv_sem=cr_sem,
        device_id={"blk": before}, device_id_type=MESH)
    send_q = []
    for h in range(HALVES):
        piece = pl.ds(h * part_rows, part_rows)
        send_q.append(pltpu.make_async_remote_copy(
            src_ref=q_v.at[piece], dst_ref=qn_v.at[piece], send_sem=qs_sem.at[h], recv_sem=qr_sem.at[h],
            device_id={"blk": before}, device_id_type=MESH))

    def send_queries():
        @pl.when(z == 0)
        def _():
            pl.semaphore_wait(barrier, 1)

        @pl.when(z != 0)
        def _():
            pl.semaphore_wait(barrier, 2)

        send_c.start()
        for copy in send_q:
            copy.start()

    far = lax.rem(b, ROW) == 0
    pl.when(has_before & jnp.logical_not(far))(send_queries)

    home_columns = down(c_home)
    own_columns = down(norm)
    low_columns = down((lane - pos).astype(jnp.float32))

    ins[3].wait()
    query = q_v[...]
    for g in range(HOME):
        first = g * home_lines
        best = best_of(query, home_columns, k_v, first * 128, home_lines * 128)
        j = key_index(first, home_lines)
        home_v[first : first + home_lines, :] = jnp.where((j >= low_home) & (j < start), best, NEG)
        if g == 0:
            pl.when(has_before & far)(send_queries)

    here = pl.ds(pl.multiple_of(start, 128), rows)
    score = dot_rows(query, k_v[here, :])
    wide = rows // 128
    score = score - jnp.concatenate([own_columns] * wide, axis=1)
    j = lax.broadcasted_iota(jnp.int32, (rows, rows), 1)
    r = lax.broadcasted_iota(jnp.int32, (rows, rows), 0)
    low = jnp.concatenate([low_columns] * wide, axis=1)
    score = jnp.where((j <= r) & (j.astype(jnp.float32) >= low), score, NEG)
    own = dense(eighths(score))
    mine = pl.ds(z * wide, wide)
    home_v[mine, :] = jnp.maximum(home_v[mine, :], own)

    @pl.when(has_after)
    def _():
        send_c.wait_recv()

    @pl.when(jnp.logical_not(has_after))
    def _():
        cn_v[...] = cs_v[...]
        qn_v[...] = q_v[...]

    cn = cn_v[...]
    next_columns = down(cn[0:1, :])
    low_n = jnp.where(has_after, cn[1:2, 0:1], jnp.float32(4 * n_keys)).astype(jnp.int32)

    def next_best(h, first, lines):
        some = next_columns[h * part_rows : (h + 1) * part_rows, :]
        best = best_of(qn_v[h * part_rows : (h + 1) * part_rows, :], some, k_v, first * 128, lines * 128)
        return jnp.maximum(
            home_v[first : first + lines, :], jnp.where(key_index(first, lines) >= low_n, best, NEG))

    for h in range(HALVES - 1):
        @pl.when(has_after)
        def _():
            send_q[h].wait_recv()

        for _, (first, lines) in cuts:
            home_v[first : first + lines, :] = next_best(h, first, lines)

    @pl.when(has_after)
    def _():
        send_q[HALVES - 1].wait_recv()

    def reduce_copy(g, sem):
        return pltpu.make_async_remote_copy(
            src_ref=part_v[g], dst_ref=recv_v[g].at[slot], send_sem=rs_send.at[g], recv_sem=sem.at[g],
            device_id={"qsub": 0}, device_id_type=MESH)

    def give(p, at):
        return [
            pltpu.make_async_remote_copy(
                src_ref=ref, dst_ref=ref, send_sem=ag_send.at[2 * at + i], recv_sem=ag_recv.at[i],
                device_id={"qsub": p}, device_id_type=MESH)
            for i, ref in enumerate((bound_v, code_v))
        ]

    def pass_on(source, done):
        for at, p in enumerate(sends[source]):
            for copy in give(p, at):
                if done:
                    copy.wait_send()
                else:
                    copy.start()

    @pl.when(z == 0)
    def _():
        for g, (first, lines) in cuts:
            recv_v[g][turn] = next_best(HALVES - 1, first, lines)
        for g, _ in cuts:
            arrived = recv_v[g].at[pl.ds(0, first_late - 1)]
            pltpu.make_async_copy(arrived, arrived, rs_early.at[g]).wait()
            mid_v[g][...] = jnp.max(recv_v[g][0:first_late], axis=0)
        full = []
        for g, _ in cuts:
            arrived = recv_v[g].at[pl.ds(first_late, n_late)]
            pltpu.make_async_copy(arrived, arrived, rs_late.at[g]).wait()
            full.append(jnp.maximum(mid_v[g][...], jnp.max(recv_v[g][first_late:n_z], axis=0)) * scale)
        code, bounds = encode(jnp.concatenate(full, axis=0))
        code_v[...] = code
        bound_v[...] = bounds

    @pl.when(z != 0)
    def _():
        @pl.when(jnp.logical_not(has_before))
        def _():
            pl.semaphore_wait(barrier, 1)

        late = (z >= n_z // 2) & (z < n_z // 2 + n_late)
        for g, (first, lines) in cuts:
            part_v[g][...] = next_best(HALVES - 1, first, lines)

            @pl.when(late)
            def _():
                reduce_copy(g, rs_late).start()

            @pl.when(jnp.logical_not(late))
            def _():
                reduce_copy(g, rs_early).start()

        for copy in give(0, 0):
            copy.wait_recv()

    for source in sends:
        pl.when(z == source)(functools.partial(pass_on, source, False))

    for source in sends:
        pl.when(z == source)(functools.partial(pass_on, source, True))

    @pl.when(z != 0)
    def _():
        for g, _ in cuts:
            reduce_copy(g, rs_early).wait_send()

    @pl.when(has_before)
    def _():
        send_c.wait_send()
        for copy in send_q:
            copy.wait_send()


def solution(mesh):
    n_blk, n_z = mesh.shape["blk"], mesh.shape["qsub"]

    def body(queries, key_rows, log_norms, positions):
        rows, head = queries.shape
        n_keys = key_rows.shape[0]
        pieces = [lines for _, lines in cut(n_keys)]
        f32 = jnp.float32
        dma = pltpu.SemaphoreType.DMA
        operands = [
            pltpu.with_memory_space_constraint(x, pltpu.HBM) for x in (queries, key_rows, log_norms, positions)
        ]
        code, bounds = pl.pallas_call(
            functools.partial(kernel, n_blk, n_z, head ** -0.5),
            out_shape=(pltpu.VMEM((n_keys // 128, 128), jnp.int16), pltpu.VMEM((2, 128), f32)),
            in_specs=[pl.BlockSpec(memory_space=pl.ANY)] * 4,
            out_specs=[pl.BlockSpec(memory_space=pltpu.VMEM)] * 2,
            scratch_shapes=[
                pltpu.VMEM((rows, head), jnp.bfloat16),
                pltpu.VMEM((n_keys, head), jnp.bfloat16),
                pltpu.VMEM((rows,), jnp.bfloat16),
                pltpu.VMEM((rows,), jnp.int32),
                pltpu.VMEM((rows, head), jnp.bfloat16),
                pltpu.VMEM((2, rows), f32),
                pltpu.VMEM((2, rows), f32),
                pltpu.VMEM((n_keys // 128, 128), f32),
                *[pltpu.VMEM((lines, 128), f32) for lines in pieces],
                *[pltpu.VMEM((n_z, lines, 128), f32) for lines in pieces],
                *[pltpu.VMEM((lines, 128), f32) for lines in pieces],
                dma((4,)), dma((HALVES,)), dma((HALVES,)), dma, dma,
                dma((len(pieces),)), dma((len(pieces),)), dma((len(pieces),)), dma((2 * n_z,)), dma((2,)),
            ],
            compiler_params=pltpu.CompilerParams(
                collective_id=0, has_side_effects=True, vmem_limit_bytes=16 * 1024 * 1024),
        )(*operands)
        return decode(code, bounds).reshape(n_keys)

    in_specs = (P(("blk", "qsub"), None), P("blk", None), P(("blk", "qsub")), P(("blk", "qsub")))
    return jax.shard_map(body, mesh=mesh, in_specs=in_specs, out_specs=P("blk"), check_vma=False)
```

```python
import functools

import jax
import jax.numpy as jnp
from jax import lax
from jax.experimental import pallas as pl
from jax.experimental.pallas import tpu as pltpu
from jax.sharding import PartitionSpec as P

MESH = pl.DeviceIdType.MESH
NEG = -1e30
FAR = 1e30
TILE = 256
HALVES = 2
PIECES = (2, 1)
HOME = 3
ROW = 8
STEPS = 65000.0


def plan(n_z):
    if n_z == 16:
        last = [8, 9, 10, 11, 12, 13, 14]
        even = {0: [1, 4, 2, 5, 3, 15], 4: [6], 5: [7], 15: last}
        return (even, {0: [1, 4, 2, 15, 3], 4: [5, 6, 7], 15: last}), 4
    return ({0: list(range(1, n_z))},) * 2, 1


def dot_rows(left, right):
    return lax.dot_general(left, right, (((1,), (1,)), ((), ())), preferred_element_type=jnp.float32)


def down(row):
    return jnp.transpose(jnp.broadcast_to(row, (128, row.shape[1])))


def fold(groups):
    number = len(groups)
    groups = groups + [groups[-1]] * (8 - number)
    row = lax.broadcasted_iota(jnp.int32, (8, 128), 0)
    for by in (4, 2, 1):
        upper = (row & by) == 0
        groups = [
            jnp.where(
                upper,
                jnp.maximum(groups[i], pltpu.roll(groups[i], 8 - by, 0)),
                jnp.maximum(groups[i + by], pltpu.roll(groups[i + by], by, 0)),
            )
            for i in range(by)
        ]
    return groups[0] if number == 8 else groups[0][:number]


def dense(groups):
    return jnp.concatenate([fold(groups[i : i + 8]) for i in range(0, len(groups), 8)], axis=0)


def eighths(score):
    rows, width = score.shape
    best = jnp.max(score.reshape(rows // 8, 8, width), axis=0)
    return [best[:, i : i + 128] for i in range(0, width, 128)]


def best_of(query, columns, k_ref, first, width):
    groups = []
    for at in range(first, first + width, TILE):
        score = dot_rows(query, k_ref[at : at + TILE, :])
        score = score - jnp.concatenate([columns] * (TILE // 128), axis=1)
        groups += eighths(score)
    return dense(groups)


def key_index(first, lines):
    line = lax.broadcasted_iota(jnp.int32, (lines, 128), 0) + first
    return line * 128 + lax.broadcasted_iota(jnp.int32, (lines, 128), 1)


def cut(n_keys):
    unit = n_keys // 128 // sum(PIECES)
    return [(sum(PIECES[:g]) * unit, PIECES[g] * unit) for g in range(len(PIECES))]


def encode(best):
    low = jnp.min(best, axis=0, keepdims=True)
    span = jnp.maximum(jnp.max(best, axis=0, keepdims=True) - low, 1e-6)
    steps = jnp.round((best - low) * (STEPS / span)) - STEPS / 2
    return steps.astype(jnp.int32).astype(jnp.int16), jnp.concatenate([low, span * (1.0 / STEPS)], axis=0)


def decode(code, bounds):
    steps = code.astype(jnp.int32).astype(jnp.float32) + STEPS / 2
    return steps * bounds[1:2, :] + bounds[0:1, :]


def kernel(
    n_blk, n_z, scale,
    q_hbm, k_hbm, ln_hbm, pos_hbm, code_v, bound_v,
    q_v, k_v, ln_v, pos_v, qn_v, cs_v, cn_v,
    home_v, part_0, part_1, recv_0, recv_1, mid_0, mid_1,
    in_sem, qs_sem, qr_sem, cs_sem, cr_sem, rs_send, rs_early, rs_late, ag_send, ag_recv,
):
    b = lax.axis_index("blk")
    z = lax.axis_index("qsub")
    sends, n_late = plan(n_z)
    rows = q_v.shape[0]
    n_keys = k_v.shape[0]
    cuts = list(enumerate(cut(n_keys)))
    part_v, recv_v, mid_v = (part_0, part_1), (recv_0, recv_1), (mid_0, mid_1)
    home_lines = n_keys // 128 // HOME
    part_rows = rows // HALVES
    before = lax.rem(b + n_blk - 1, n_blk)
    after = lax.rem(b + 1, n_blk)
    has_before = b > 0
    has_after = b < n_blk - 1
    turn = n_z // 2 - n_late
    slot = lax.rem(z + turn, n_z)
    first_late = n_z - n_late

    barrier = pltpu.get_barrier_semaphore()

    @pl.when(has_after)
    def _():
        pl.semaphore_signal(barrier, inc=1, device_id={"blk": after}, device_id_type=MESH)

    @pl.when(z == 0)
    def _():
        for p in range(1, n_z):
            pl.semaphore_signal(barrier, inc=1, device_id={"qsub": p}, device_id_type=MESH)

    ins = [
        pltpu.make_async_copy(ln_hbm, ln_v, in_sem.at[0]),
        pltpu.make_async_copy(pos_hbm, pos_v, in_sem.at[1]),
        pltpu.make_async_copy(q_hbm, q_v, in_sem.at[2]),
        pltpu.make_async_copy(k_hbm, k_v, in_sem.at[3]),
    ]
    for copy in ins:
        copy.start()
    ins[0].wait()
    ins[1].wait()

    start = z * rows
    lane = lax.broadcasted_iota(jnp.int32, (1, rows), 1)
    pos = pos_v[...].reshape(1, rows)
    norm = ln_v[...].astype(jnp.float32).reshape(1, rows) * (1.0 / scale)
    first_pos = pos[:, 0:1]
    c_home = jnp.where(pos > lane, norm, FAR)
    c_next = jnp.where(pos > lane + start, norm, FAR)
    low_home = start - first_pos
    low_next = n_keys + start - first_pos
    cs_v[0:1, :] = c_next
    cs_v[1:2, :] = jnp.broadcast_to(low_next.astype(jnp.float32), (1, rows))
    ins[2].wait()

    send_c = pltpu.make_async_remote_copy(
        src_ref=cs_v, dst_ref=cn_v, send_sem=cs_sem, recv_sem=cr_sem,
        device_id={"blk": before}, device_id_type=MESH)
    send_q = []
    for h in range(HALVES):
        piece = pl.ds(h * part_rows, part_rows)
        send_q.append(pltpu.make_async_remote_copy(
            src_ref=q_v.at[piece], dst_ref=qn_v.at[piece], send_sem=qs_sem.at[h], recv_sem=qr_sem.at[h],
            device_id={"blk": before}, device_id_type=MESH))

    def send_queries():
        @pl.when(z == 0)
        def _():
            pl.semaphore_wait(barrier, 1)

        @pl.when(z != 0)
        def _():
            pl.semaphore_wait(barrier, 2)

        send_c.start()
        for copy in send_q:
            copy.start()

    far = lax.rem(b, ROW) == 0
    pl.when(has_before & jnp.logical_not(far))(send_queries)

    home_columns = down(c_home)
    own_columns = down(norm)
    low_columns = down((lane - pos).astype(jnp.float32))

    ins[3].wait()
    query = q_v[...]
    for g in range(HOME):
        first = g * home_lines
        best = best_of(query, home_columns, k_v, first * 128, home_lines * 128)
        j = key_index(first, home_lines)
        home_v[first : first + home_lines, :] = jnp.where((j >= low_home) & (j < start), best, NEG)
        if g == 0:
            pl.when(has_before & far)(send_queries)

    here = pl.ds(pl.multiple_of(start, 128), rows)
    score = dot_rows(query, k_v[here, :])
    wide = rows // 128
    score = score - jnp.concatenate([own_columns] * wide, axis=1)
    j = lax.broadcasted_iota(jnp.int32, (rows, rows), 1)
    r = lax.broadcasted_iota(jnp.int32, (rows, rows), 0)
    low = jnp.concatenate([low_columns] * wide, axis=1)
    score = jnp.where((j <= r) & (j.astype(jnp.float32) >= low), score, NEG)
    own = dense(eighths(score))
    mine = pl.ds(z * wide, wide)
    home_v[mine, :] = jnp.maximum(home_v[mine, :], own)

    @pl.when(has_after)
    def _():
        send_c.wait_recv()

    @pl.when(jnp.logical_not(has_after))
    def _():
        cn_v[...] = cs_v[...]
        qn_v[...] = q_v[...]

    cn = cn_v[...]
    next_columns = down(cn[0:1, :])
    low_n = jnp.where(has_after, cn[1:2, 0:1], jnp.float32(4 * n_keys)).astype(jnp.int32)

    def next_best(h, first, lines):
        some = next_columns[h * part_rows : (h + 1) * part_rows, :]
        best = best_of(qn_v[h * part_rows : (h + 1) * part_rows, :], some, k_v, first * 128, lines * 128)
        return jnp.maximum(
            home_v[first : first + lines, :], jnp.where(key_index(first, lines) >= low_n, best, NEG))

    for h in range(HALVES - 1):
        @pl.when(has_after)
        def _():
            send_q[h].wait_recv()

        for _, (first, lines) in cuts:
            home_v[first : first + lines, :] = next_best(h, first, lines)

    @pl.when(has_after)
    def _():
        send_q[HALVES - 1].wait_recv()

    def reduce_copy(g, sem):
        return pltpu.make_async_remote_copy(
            src_ref=part_v[g], dst_ref=recv_v[g].at[slot], send_sem=rs_send.at[g], recv_sem=sem.at[g],
            device_id={"qsub": 0}, device_id_type=MESH)

    def give(p, at):
        return [
            pltpu.make_async_remote_copy(
                src_ref=ref, dst_ref=ref, send_sem=ag_send.at[2 * at + i], recv_sem=ag_recv.at[i],
                device_id={"qsub": p}, device_id_type=MESH)
            for i, ref in enumerate((bound_v, code_v))
        ]

    def pass_on(targets, done):
        for at, p in enumerate(targets):
            for copy in give(p, at):
                if done:
                    copy.wait_send()
                else:
                    copy.start()

    @pl.when(z == 0)
    def _():
        for g, (first, lines) in cuts:
            recv_v[g][turn] = next_best(HALVES - 1, first, lines)
        for g, _ in cuts:
            arrived = recv_v[g].at[pl.ds(0, first_late - 1)]
            pltpu.make_async_copy(arrived, arrived, rs_early.at[g]).wait()
            mid_v[g][...] = jnp.max(recv_v[g][0:first_late], axis=0)
        full = []
        for g, _ in cuts:
            arrived = recv_v[g].at[pl.ds(first_late, n_late)]
            pltpu.make_async_copy(arrived, arrived, rs_late.at[g]).wait()
            full.append(jnp.maximum(mid_v[g][...], jnp.max(recv_v[g][first_late:n_z], axis=0)) * scale)
        code, bounds = encode(jnp.concatenate(full, axis=0))
        code_v[...] = code
        bound_v[...] = bounds

    @pl.when(z != 0)
    def _():
        @pl.when(jnp.logical_not(has_before))
        def _():
            pl.semaphore_wait(barrier, 1)

        late = (z >= n_z // 2) & (z < n_z // 2 + n_late)
        for g, (first, lines) in cuts:
            part_v[g][...] = next_best(HALVES - 1, first, lines)

            @pl.when(late)
            def _():
                reduce_copy(g, rs_late).start()

            @pl.when(jnp.logical_not(late))
            def _():
                reduce_copy(g, rs_early).start()

        for copy in give(0, 0):
            copy.wait_recv()

    givers = [
        ((z == source) & (lax.rem(b, 2) == odd), targets)
        for odd in range(2)
        for source, targets in sends[odd].items()
    ]
    for gives, targets in givers:
        pl.when(gives)(functools.partial(pass_on, targets, False))

    for gives, targets in givers:
        pl.when(gives)(functools.partial(pass_on, targets, True))

    @pl.when(z != 0)
    def _():
        for g, _ in cuts:
            reduce_copy(g, rs_early).wait_send()

    @pl.when(has_before)
    def _():
        send_c.wait_send()
        for copy in send_q:
            copy.wait_send()


def solution(mesh):
    n_blk, n_z = mesh.shape["blk"], mesh.shape["qsub"]

    def body(queries, key_rows, log_norms, positions):
        rows, head = queries.shape
        n_keys = key_rows.shape[0]
        pieces = [lines for _, lines in cut(n_keys)]
        f32 = jnp.float32
        dma = pltpu.SemaphoreType.DMA
        operands = [
            pltpu.with_memory_space_constraint(x, pltpu.HBM) for x in (queries, key_rows, log_norms, positions)
        ]
        code, bounds = pl.pallas_call(
            functools.partial(kernel, n_blk, n_z, head ** -0.5),
            out_shape=(pltpu.VMEM((n_keys // 128, 128), jnp.int16), pltpu.VMEM((2, 128), f32)),
            in_specs=[pl.BlockSpec(memory_space=pl.ANY)] * 4,
            out_specs=[pl.BlockSpec(memory_space=pltpu.VMEM)] * 2,
            scratch_shapes=[
                pltpu.VMEM((rows, head), jnp.bfloat16),
                pltpu.VMEM((n_keys, head), jnp.bfloat16),
                pltpu.VMEM((rows,), jnp.bfloat16),
                pltpu.VMEM((rows,), jnp.int32),
                pltpu.VMEM((rows, head), jnp.bfloat16),
                pltpu.VMEM((2, rows), f32),
                pltpu.VMEM((2, rows), f32),
                pltpu.VMEM((n_keys // 128, 128), f32),
                *[pltpu.VMEM((lines, 128), f32) for lines in pieces],
                *[pltpu.VMEM((n_z, lines, 128), f32) for lines in pieces],
                *[pltpu.VMEM((lines, 128), f32) for lines in pieces],
                dma((4,)), dma((HALVES,)), dma((HALVES,)), dma, dma,
                dma((len(pieces),)), dma((len(pieces),)), dma((len(pieces),)), dma((2 * n_z,)), dma((2,)),
            ],
            compiler_params=pltpu.CompilerParams(
                collective_id=0, has_side_effects=True, vmem_limit_bytes=16 * 1024 * 1024),
        )(*operands)
        return decode(code, bounds).reshape(n_keys)

    in_specs = (P(("blk", "qsub"), None), P("blk", None), P(("blk", "qsub")), P(("blk", "qsub")))
    return jax.shard_map(body, mesh=mesh, in_specs=in_specs, out_specs=P("blk"), check_vma=False)
```

```python
import functools

import jax
import jax.numpy as jnp
from jax import lax
from jax.experimental import pallas as pl
from jax.experimental.pallas import tpu as pltpu
from jax.sharding import PartitionSpec as P

MESH = pl.DeviceIdType.MESH
NEG = -1e30
FAR = 1e30
TILE = 256
HALVES = 2
PIECES = (2, 1)
HOME = 3
ROW = 8
STEPS = 65000.0


def plan(n_z):
    if n_z == 16:
        last = [8, 9, 10, 11, 12, 13, 14]
        even = {0: [1, 4, 2, 5, 3, 15], 4: [6], 5: [7], 15: last}
        return (even, {0: [1, 4, 2, 15, 3], 4: [5, 6, 7], 15: last}), 4
    return ({0: list(range(1, n_z))},) * 2, 1


def dot_rows(left, right):
    return lax.dot_general(left, right, (((1,), (1,)), ((), ())), preferred_element_type=jnp.float32)


def down(row):
    return jnp.transpose(jnp.broadcast_to(row, (128, row.shape[1])))


def fold(groups):
    number = len(groups)
    groups = groups + [groups[-1]] * (8 - number)
    row = lax.broadcasted_iota(jnp.int32, (8, 128), 0)
    for by in (4, 2, 1):
        upper = (row & by) == 0
        groups = [
            jnp.where(
                upper,
                jnp.maximum(groups[i], pltpu.roll(groups[i], 8 - by, 0)),
                jnp.maximum(groups[i + by], pltpu.roll(groups[i + by], by, 0)),
            )
            for i in range(by)
        ]
    return groups[0] if number == 8 else groups[0][:number]


def dense(groups):
    return jnp.concatenate([fold(groups[i : i + 8]) for i in range(0, len(groups), 8)], axis=0)


def eighths(score):
    rows, width = score.shape
    best = jnp.max(score.reshape(rows // 8, 8, width), axis=0)
    return [best[:, i : i + 128] for i in range(0, width, 128)]


def best_of(query, columns, k_ref, first, width):
    groups = []
    for at in range(first, first + width, TILE):
        score = dot_rows(query, k_ref[at : at + TILE, :])
        score = score - jnp.concatenate([columns] * (TILE // 128), axis=1)
        groups += eighths(score)
    return dense(groups)


def key_index(first, lines):
    line = lax.broadcasted_iota(jnp.int32, (lines, 128), 0) + first
    return line * 128 + lax.broadcasted_iota(jnp.int32, (lines, 128), 1)


def cut(n_keys):
    unit = n_keys // 128 // sum(PIECES)
    return [(sum(PIECES[:g]) * unit, PIECES[g] * unit) for g in range(len(PIECES))]


def encode(best):
    low = jnp.min(best, axis=0, keepdims=True)
    span = jnp.maximum(jnp.max(best, axis=0, keepdims=True) - low, 1e-6)
    steps = jnp.round((best - low) * (STEPS / span)) - STEPS / 2
    return steps.astype(jnp.int32).astype(jnp.int16), jnp.concatenate([low, span * (1.0 / STEPS)], axis=0)


def decode(code, bounds):
    steps = code.astype(jnp.int32).astype(jnp.float32) + STEPS / 2
    return steps * bounds[1:2, :] + bounds[0:1, :]


def kernel(
    n_blk, n_z, scale,
    q_hbm, k_hbm, ln_hbm, pos_hbm, code_v, bound_v,
    q_v, k_v, ln_v, pos_v, qn_v, cs_v, cn_v,
    home_v, part_0, part_1, recv_0, recv_1, mid_0, mid_1,
    in_sem, qs_sem, qr_sem, cs_sem, cr_sem, rs_send, rs_recv, ag_send, ag_recv,
):
    b = lax.axis_index("blk")
    z = lax.axis_index("qsub")
    sends, n_late = plan(n_z)
    rows = q_v.shape[0]
    n_keys = k_v.shape[0]
    cuts = list(enumerate(cut(n_keys)))
    part_v, recv_v, mid_v = (part_0, part_1), (recv_0, recv_1), (mid_0, mid_1)
    home_lines = n_keys // 128 // HOME
    part_rows = rows // HALVES
    before = lax.rem(b + n_blk - 1, n_blk)
    after = lax.rem(b + 1, n_blk)
    has_before = b > 0
    has_after = b < n_blk - 1
    turn = n_z // 2 - n_late
    slot = lax.rem(z + turn, n_z)
    first_late = n_z - n_late

    barrier = pltpu.get_barrier_semaphore()

    @pl.when(has_after)
    def _():
        pl.semaphore_signal(barrier, inc=1, device_id={"blk": after}, device_id_type=MESH)

    @pl.when(z == 0)
    def _():
        for p in range(1, n_z):
            pl.semaphore_signal(barrier, inc=1, device_id={"qsub": p}, device_id_type=MESH)

    ins = [
        pltpu.make_async_copy(ln_hbm, ln_v, in_sem.at[0]),
        pltpu.make_async_copy(pos_hbm, pos_v, in_sem.at[1]),
        pltpu.make_async_copy(q_hbm, q_v, in_sem.at[2]),
        pltpu.make_async_copy(k_hbm, k_v, in_sem.at[3]),
    ]
    for copy in ins:
        copy.start()
    ins[0].wait()
    ins[1].wait()

    start = z * rows
    lane = lax.broadcasted_iota(jnp.int32, (1, rows), 1)
    pos = pos_v[...].reshape(1, rows)
    norm = ln_v[...].astype(jnp.float32).reshape(1, rows) * (1.0 / scale)
    first_pos = pos[:, 0:1]
    c_home = jnp.where(pos > lane, norm, FAR)
    c_next = jnp.where(pos > lane + start, norm, FAR)
    low_home = start - first_pos
    low_next = n_keys + start - first_pos
    cs_v[0:1, :] = c_next
    cs_v[1:2, :] = jnp.broadcast_to(low_next.astype(jnp.float32), (1, rows))
    ins[2].wait()

    send_c = pltpu.make_async_remote_copy(
        src_ref=cs_v, dst_ref=cn_v, send_sem=cs_sem, recv_sem=cr_sem,
        device_id={"blk": before}, device_id_type=MESH)
    send_q = []
    for h in range(HALVES):
        piece = pl.ds(h * part_rows, part_rows)
        send_q.append(pltpu.make_async_remote_copy(
            src_ref=q_v.at[piece], dst_ref=qn_v.at[piece], send_sem=qs_sem.at[h], recv_sem=qr_sem.at[h],
            device_id={"blk": before}, device_id_type=MESH))

    def send_queries():
        @pl.when(z == 0)
        def _():
            pl.semaphore_wait(barrier, 1)

        @pl.when(z != 0)
        def _():
            pl.semaphore_wait(barrier, 2)

        send_c.start()
        for copy in send_q:
            copy.start()

    far = lax.rem(b, ROW) == 0
    pl.when(has_before & jnp.logical_not(far))(send_queries)

    home_columns = down(c_home)
    own_columns = down(norm)
    low_columns = down((lane - pos).astype(jnp.float32))

    ins[3].wait()
    query = q_v[...]
    for g in range(HOME):
        first = g * home_lines
        best = best_of(query, home_columns, k_v, first * 128, home_lines * 128)
        j = key_index(first, home_lines)
        home_v[first : first + home_lines, :] = jnp.where((j >= low_home) & (j < start), best, NEG)
        if g == 0:
            pl.when(has_before & far)(send_queries)

    here = pl.ds(pl.multiple_of(start, 128), rows)
    score = dot_rows(query, k_v[here, :])
    wide = rows // 128
    score = score - jnp.concatenate([own_columns] * wide, axis=1)
    j = lax.broadcasted_iota(jnp.int32, (rows, rows), 1)
    r = lax.broadcasted_iota(jnp.int32, (rows, rows), 0)
    low = jnp.concatenate([low_columns] * wide, axis=1)
    score = jnp.where((j <= r) & (j.astype(jnp.float32) >= low), score, NEG)
    own = dense(eighths(score))
    mine = pl.ds(z * wide, wide)
    home_v[mine, :] = jnp.maximum(home_v[mine, :], own)

    @pl.when(has_after)
    def _():
        send_c.wait_recv()

    @pl.when(jnp.logical_not(has_after))
    def _():
        cn_v[...] = cs_v[...]
        qn_v[...] = q_v[...]

    cn = cn_v[...]
    next_columns = down(cn[0:1, :])
    low_n = jnp.where(has_after, cn[1:2, 0:1], jnp.float32(4 * n_keys)).astype(jnp.int32)

    def next_best(h, first, lines):
        some = next_columns[h * part_rows : (h + 1) * part_rows, :]
        best = best_of(qn_v[h * part_rows : (h + 1) * part_rows, :], some, k_v, first * 128, lines * 128)
        return jnp.maximum(
            home_v[first : first + lines, :], jnp.where(key_index(first, lines) >= low_n, best, NEG))

    for h in range(HALVES - 1):
        @pl.when(has_after)
        def _():
            send_q[h].wait_recv()

        for _, (first, lines) in cuts:
            home_v[first : first + lines, :] = next_best(h, first, lines)

    @pl.when(has_after)
    def _():
        send_q[HALVES - 1].wait_recv()

    group = ((z >= n_z // 2) & (z < n_z // 2 + n_late)).astype(jnp.int32)

    def reduce_copy(g):
        return pltpu.make_async_remote_copy(
            src_ref=part_v[g], dst_ref=recv_v[g].at[slot], send_sem=rs_send.at[g], recv_sem=rs_recv.at[group * len(cuts) + g],
            device_id={"qsub": 0}, device_id_type=MESH)

    def give(p, at):
        return [
            pltpu.make_async_remote_copy(
                src_ref=ref, dst_ref=ref, send_sem=ag_send.at[2 * at + i], recv_sem=ag_recv.at[i],
                device_id={"qsub": p}, device_id_type=MESH)
            for i, ref in enumerate((bound_v, code_v))
        ]

    def pass_on(targets, done):
        for at, p in enumerate(targets):
            for copy in give(p, at):
                if done:
                    copy.wait_send()
                else:
                    copy.start()

    @pl.when(z == 0)
    def _():
        for g, (first, lines) in cuts:
            recv_v[g][turn] = next_best(HALVES - 1, first, lines)
        for g, _ in cuts:
            arrived = recv_v[g].at[pl.ds(0, first_late - 1)]
            pltpu.make_async_copy(arrived, arrived, rs_recv.at[g]).wait()
            mid_v[g][...] = jnp.max(recv_v[g][0:first_late], axis=0)
        full = []
        for g, _ in cuts:
            arrived = recv_v[g].at[pl.ds(first_late, n_late)]
            pltpu.make_async_copy(arrived, arrived, rs_recv.at[len(cuts) + g]).wait()
            full.append(jnp.maximum(mid_v[g][...], jnp.max(recv_v[g][first_late:n_z], axis=0)) * scale)
        code, bounds = encode(jnp.concatenate(full, axis=0))
        code_v[...] = code
        bound_v[...] = bounds

    @pl.when(z != 0)
    def _():
        @pl.when(jnp.logical_not(has_before))
        def _():
            pl.semaphore_wait(barrier, 1)

        for g, (first, lines) in cuts:
            part_v[g][...] = next_best(HALVES - 1, first, lines)
            reduce_copy(g).start()

        for copy in give(0, 0):
            copy.wait_recv()

    givers = [
        ((z == source) & (lax.rem(b, 2) == odd), targets)
        for odd in range(2)
        for source, targets in sends[odd].items()
    ]
    for gives, targets in givers:
        pl.when(gives)(functools.partial(pass_on, targets, False))

    for gives, targets in givers:
        pl.when(gives)(functools.partial(pass_on, targets, True))

    @pl.when(z != 0)
    def _():
        for g, _ in cuts:
            reduce_copy(g).wait_send()

    @pl.when(has_before)
    def _():
        send_c.wait_send()
        for copy in send_q:
            copy.wait_send()


def solution(mesh):
    n_blk, n_z = mesh.shape["blk"], mesh.shape["qsub"]

    def body(queries, key_rows, log_norms, positions):
        rows, head = queries.shape
        n_keys = key_rows.shape[0]
        pieces = [lines for _, lines in cut(n_keys)]
        f32 = jnp.float32
        dma = pltpu.SemaphoreType.DMA
        operands = [
            pltpu.with_memory_space_constraint(x, pltpu.HBM) for x in (queries, key_rows, log_norms, positions)
        ]
        code, bounds = pl.pallas_call(
            functools.partial(kernel, n_blk, n_z, head ** -0.5),
            out_shape=(pltpu.VMEM((n_keys // 128, 128), jnp.int16), pltpu.VMEM((2, 128), f32)),
            in_specs=[pl.BlockSpec(memory_space=pl.ANY)] * 4,
            out_specs=[pl.BlockSpec(memory_space=pltpu.VMEM)] * 2,
            scratch_shapes=[
                pltpu.VMEM((rows, head), jnp.bfloat16),
                pltpu.VMEM((n_keys, head), jnp.bfloat16),
                pltpu.VMEM((rows,), jnp.bfloat16),
                pltpu.VMEM((rows,), jnp.int32),
                pltpu.VMEM((rows, head), jnp.bfloat16),
                pltpu.VMEM((2, rows), f32),
                pltpu.VMEM((2, rows), f32),
                pltpu.VMEM((n_keys // 128, 128), f32),
                *[pltpu.VMEM((lines, 128), f32) for lines in pieces],
                *[pltpu.VMEM((n_z, lines, 128), f32) for lines in pieces],
                *[pltpu.VMEM((lines, 128), f32) for lines in pieces],
                dma((4,)), dma((HALVES,)), dma((HALVES,)), dma, dma,
                dma((len(pieces),)), dma((2 * len(pieces),)), dma((2 * n_z,)), dma((2,)),
            ],
            compiler_params=pltpu.CompilerParams(
                collective_id=0, has_side_effects=True, vmem_limit_bytes=16 * 1024 * 1024),
        )(*operands)
        return decode(code, bounds).reshape(n_keys)

    in_specs = (P(("blk", "qsub"), None), P("blk", None), P(("blk", "qsub")), P(("blk", "qsub")))
    return jax.shard_map(body, mesh=mesh, in_specs=in_specs, out_specs=P("blk"), check_vma=False)
```

```python
import functools

import jax
import jax.numpy as jnp
from jax import lax
from jax.experimental import pallas as pl
from jax.experimental.pallas import tpu as pltpu
from jax.sharding import PartitionSpec as P

MESH = pl.DeviceIdType.MESH
NEG = -1e30
FAR = 1e30
TILE = 256
HALVES = 2
PIECES = (2, 1)
HOME = 3
ROW = 8
STEPS = 65000.0


def plan(n_z):
    if n_z == 16:
        last = [8, 9, 10, 11, 12, 13, 14]
        even = {0: [1, 4, 2, 5, 3, 15], 4: [6], 5: [7], 15: last}
        return (even, {0: [1, 4, 2, 15, 3], 4: [5, 6, 7], 15: last}), 4
    return ({0: list(range(1, n_z))},) * 2, 1


def dot_rows(left, right):
    return lax.dot_general(left, right, (((1,), (1,)), ((), ())), preferred_element_type=jnp.float32)


def down(row):
    return jnp.transpose(jnp.broadcast_to(row, (128, row.shape[1])))


def fold(groups):
    number = len(groups)
    groups = groups + [groups[-1]] * (8 - number)
    row = lax.broadcasted_iota(jnp.int32, (8, 128), 0)
    for by in (4, 2, 1):
        upper = (row & by) == 0
        groups = [
            jnp.where(
                upper,
                jnp.maximum(groups[i], pltpu.roll(groups[i], 8 - by, 0)),
                jnp.maximum(groups[i + by], pltpu.roll(groups[i + by], by, 0)),
            )
            for i in range(by)
        ]
    return groups[0] if number == 8 else groups[0][:number]


def dense(groups):
    return jnp.concatenate([fold(groups[i : i + 8]) for i in range(0, len(groups), 8)], axis=0)


def eighths(score):
    rows, width = score.shape
    best = jnp.max(score.reshape(rows // 8, 8, width), axis=0)
    return [best[:, i : i + 128] for i in range(0, width, 128)]


def best_of(query, columns, k_ref, first, width):
    groups = []
    for at in range(first, first + width, TILE):
        score = dot_rows(query, k_ref[at : at + TILE, :])
        score = score - jnp.concatenate([columns] * (TILE // 128), axis=1)
        groups += eighths(score)
    return dense(groups)


def key_index(first, lines):
    line = lax.broadcasted_iota(jnp.int32, (lines, 128), 0) + first
    return line * 128 + lax.broadcasted_iota(jnp.int32, (lines, 128), 1)


def cut(n_keys):
    unit = n_keys // 128 // sum(PIECES)
    return [(sum(PIECES[:g]) * unit, PIECES[g] * unit) for g in range(len(PIECES))]


def encode(best):
    low = jnp.min(best, axis=0, keepdims=True)
    span = jnp.maximum(jnp.max(best, axis=0, keepdims=True) - low, 1e-6)
    steps = jnp.round((best - low) * (STEPS / span)) - STEPS / 2
    return steps.astype(jnp.int32).astype(jnp.int16), jnp.concatenate([low, span * (1.0 / STEPS)], axis=0)


def decode(code, bounds):
    steps = code.astype(jnp.int32).astype(jnp.float32) + STEPS / 2
    return steps * bounds[1:2, :] + bounds[0:1, :]


def kernel(
    n_blk, n_z, scale,
    q_hbm, k_hbm, ln_hbm, pos_hbm, code_v, bound_v,
    q_v, k_v, ln_v, pos_v, qn_v, cs_v, cn_v,
    home_v, part_0, part_1, recv_0, recv_1, mid_0, mid_1,
    in_sem, qs_sem, qr_sem, cs_sem, cr_sem, rs_send, rs_recv, ag_send, ag_recv,
):
    b = lax.axis_index("blk")
    z = lax.axis_index("qsub")
    sends, n_late = plan(n_z)
    rows = q_v.shape[0]
    n_keys = k_v.shape[0]
    cuts = list(enumerate(cut(n_keys)))
    part_v, recv_v, mid_v = (part_0, part_1), (recv_0, recv_1), (mid_0, mid_1)
    home_lines = n_keys // 128 // HOME
    part_rows = rows // HALVES
    before = lax.rem(b + n_blk - 1, n_blk)
    after = lax.rem(b + 1, n_blk)
    has_before = b > 0
    has_after = b < n_blk - 1
    turn = n_z // 2 - n_late
    slot = lax.rem(z + turn, n_z)
    first_late = n_z - n_late

    barrier = pltpu.get_barrier_semaphore()

    @pl.when(has_after)
    def _():
        pl.semaphore_signal(barrier, inc=1, device_id={"blk": after}, device_id_type=MESH)

    @pl.when(z == 0)
    def _():
        for p in range(1, n_z):
            pl.semaphore_signal(barrier, inc=1, device_id={"qsub": p}, device_id_type=MESH)

    ins = [
        pltpu.make_async_copy(ln_hbm, ln_v, in_sem.at[0]),
        pltpu.make_async_copy(pos_hbm, pos_v, in_sem.at[1]),
        pltpu.make_async_copy(q_hbm, q_v, in_sem.at[2]),
        pltpu.make_async_copy(k_hbm, k_v, in_sem.at[3]),
    ]
    for copy in ins:
        copy.start()
    ins[0].wait()
    ins[1].wait()

    start = z * rows
    lane = lax.broadcasted_iota(jnp.int32, (1, rows), 1)
    pos = pos_v[...].reshape(1, rows)
    norm = ln_v[...].astype(jnp.float32).reshape(1, rows) * (1.0 / scale)
    first_pos = pos[:, 0:1]
    c_home = jnp.where(pos > lane, norm, FAR)
    c_next = jnp.where(pos > lane + start, norm, FAR)
    low_home = start - first_pos
    low_next = n_keys + start - first_pos
    cs_v[0:1, :] = c_next
    cs_v[1:2, :] = jnp.broadcast_to(low_next.astype(jnp.float32), (1, rows))
    ins[2].wait()

    send_c = pltpu.make_async_remote_copy(
        src_ref=cs_v, dst_ref=cn_v, send_sem=cs_sem, recv_sem=cr_sem,
        device_id={"blk": before}, device_id_type=MESH)
    send_q = []
    for h in range(HALVES):
        piece = pl.ds(h * part_rows, part_rows)
        send_q.append(pltpu.make_async_remote_copy(
            src_ref=q_v.at[piece], dst_ref=qn_v.at[piece], send_sem=qs_sem.at[h], recv_sem=qr_sem.at[h],
            device_id={"blk": before}, device_id_type=MESH))

    def send_queries():
        @pl.when(z == 0)
        def _():
            pl.semaphore_wait(barrier, 1)

        @pl.when(z != 0)
        def _():
            pl.semaphore_wait(barrier, 2)

        send_c.start()
        for copy in send_q:
            copy.start()

    far = lax.rem(b, ROW) == 0
    pl.when(has_before & jnp.logical_not(far))(send_queries)

    home_columns = down(c_home)
    own_columns = down(norm)
    low_columns = down((lane - pos).astype(jnp.float32))

    ins[3].wait()
    query = q_v[...]
    for g in range(HOME):
        first = g * home_lines
        best = best_of(query, home_columns, k_v, first * 128, home_lines * 128)
        j = key_index(first, home_lines)
        home_v[first : first + home_lines, :] = jnp.where((j >= low_home) & (j < start), best, NEG)
        if g == 0:
            pl.when(has_before & far)(send_queries)

    here = pl.ds(pl.multiple_of(start, 128), rows)
    score = dot_rows(query, k_v[here, :])
    wide = rows // 128
    score = score - jnp.concatenate([own_columns] * wide, axis=1)
    j = lax.broadcasted_iota(jnp.int32, (rows, rows), 1)
    r = lax.broadcasted_iota(jnp.int32, (rows, rows), 0)
    low = jnp.concatenate([low_columns] * wide, axis=1)
    score = jnp.where((j <= r) & (j.astype(jnp.float32) >= low), score, NEG)
    own = dense(eighths(score))
    mine = pl.ds(z * wide, wide)
    home_v[mine, :] = jnp.maximum(home_v[mine, :], own)

    @pl.when(has_after)
    def _():
        send_c.wait_recv()

    @pl.when(jnp.logical_not(has_after))
    def _():
        cn_v[...] = cs_v[...]
        qn_v[...] = q_v[...]

    cn = cn_v[...]
    next_columns = down(cn[0:1, :])
    low_n = jnp.where(has_after, cn[1:2, 0:1], jnp.float32(4 * n_keys)).astype(jnp.int32)

    def next_best(h, first, lines):
        some = next_columns[h * part_rows : (h + 1) * part_rows, :]
        best = best_of(qn_v[h * part_rows : (h + 1) * part_rows, :], some, k_v, first * 128, lines * 128)
        return jnp.maximum(
            home_v[first : first + lines, :], jnp.where(key_index(first, lines) >= low_n, best, NEG))

    @pl.when(jnp.logical_not(has_before) & (z != 0))
    def _():
        pl.semaphore_wait(barrier, 1)

    for h in range(HALVES - 1):
        @pl.when(has_after)
        def _():
            send_q[h].wait_recv()

        for _, (first, lines) in cuts:
            home_v[first : first + lines, :] = next_best(h, first, lines)

    @pl.when(has_after)
    def _():
        send_q[HALVES - 1].wait_recv()

    group = ((z >= n_z // 2) & (z < n_z // 2 + n_late)).astype(jnp.int32)

    def reduce_copy(g):
        return pltpu.make_async_remote_copy(
            src_ref=part_v[g], dst_ref=recv_v[g].at[slot], send_sem=rs_send.at[g], recv_sem=rs_recv.at[group * len(cuts) + g],
            device_id={"qsub": 0}, device_id_type=MESH)

    def give(p, at):
        return [
            pltpu.make_async_remote_copy(
                src_ref=ref, dst_ref=ref, send_sem=ag_send.at[2 * at + i], recv_sem=ag_recv.at[i],
                device_id={"qsub": p}, device_id_type=MESH)
            for i, ref in enumerate((bound_v, code_v))
        ]

    def pass_on(targets, done):
        for at, p in enumerate(targets):
            for copy in give(p, at):
                if done:
                    copy.wait_send()
                else:
                    copy.start()

    @pl.when(z == 0)
    def _():
        for g, (first, lines) in cuts:
            recv_v[g][turn] = next_best(HALVES - 1, first, lines)
        for g, _ in cuts:
            arrived = recv_v[g].at[pl.ds(0, first_late - 1)]
            pltpu.make_async_copy(arrived, arrived, rs_recv.at[g]).wait()
            mid_v[g][...] = jnp.max(recv_v[g][0:first_late], axis=0)
        full = []
        for g, _ in cuts:
            arrived = recv_v[g].at[pl.ds(first_late, n_late)]
            pltpu.make_async_copy(arrived, arrived, rs_recv.at[len(cuts) + g]).wait()
            full.append(jnp.maximum(mid_v[g][...], jnp.max(recv_v[g][first_late:n_z], axis=0)) * scale)
        code, bounds = encode(jnp.concatenate(full, axis=0))
        code_v[...] = code
        bound_v[...] = bounds

    @pl.when(z != 0)
    def _():
        for g, (first, lines) in cuts:
            part_v[g][...] = next_best(HALVES - 1, first, lines)
            reduce_copy(g).start()

        for copy in give(0, 0):
            copy.wait_recv()

    givers = [
        ((z == source) & (lax.rem(b, 2) == odd), targets)
        for odd in range(2)
        for source, targets in sends[odd].items()
    ]
    for gives, targets in givers:
        pl.when(gives)(functools.partial(pass_on, targets, False))

    for gives, targets in givers:
        pl.when(gives)(functools.partial(pass_on, targets, True))

    @pl.when(z != 0)
    def _():
        for g, _ in cuts:
            reduce_copy(g).wait_send()

    @pl.when(has_before)
    def _():
        send_c.wait_send()
        for copy in send_q:
            copy.wait_send()


def solution(mesh):
    n_blk, n_z = mesh.shape["blk"], mesh.shape["qsub"]

    def body(queries, key_rows, log_norms, positions):
        rows, head = queries.shape
        n_keys = key_rows.shape[0]
        pieces = [lines for _, lines in cut(n_keys)]
        f32 = jnp.float32
        dma = pltpu.SemaphoreType.DMA
        operands = [
            pltpu.with_memory_space_constraint(x, pltpu.HBM) for x in (queries, key_rows, log_norms, positions)
        ]
        code, bounds = pl.pallas_call(
            functools.partial(kernel, n_blk, n_z, head ** -0.5),
            out_shape=(pltpu.VMEM((n_keys // 128, 128), jnp.int16), pltpu.VMEM((2, 128), f32)),
            in_specs=[pl.BlockSpec(memory_space=pl.ANY)] * 4,
            out_specs=[pl.BlockSpec(memory_space=pltpu.VMEM)] * 2,
            scratch_shapes=[
                pltpu.VMEM((rows, head), jnp.bfloat16),
                pltpu.VMEM((n_keys, head), jnp.bfloat16),
                pltpu.VMEM((rows,), jnp.bfloat16),
                pltpu.VMEM((rows,), jnp.int32),
                pltpu.VMEM((rows, head), jnp.bfloat16),
                pltpu.VMEM((2, rows), f32),
                pltpu.VMEM((2, rows), f32),
                pltpu.VMEM((n_keys // 128, 128), f32),
                *[pltpu.VMEM((lines, 128), f32) for lines in pieces],
                *[pltpu.VMEM((n_z, lines, 128), f32) for lines in pieces],
                *[pltpu.VMEM((lines, 128), f32) for lines in pieces],
                dma((4,)), dma((HALVES,)), dma((HALVES,)), dma, dma,
                dma((len(pieces),)), dma((2 * len(pieces),)), dma((2 * n_z,)), dma((2,)),
            ],
            compiler_params=pltpu.CompilerParams(
                collective_id=0, has_side_effects=True, vmem_limit_bytes=16 * 1024 * 1024),
        )(*operands)
        return decode(code, bounds).reshape(n_keys)

    in_specs = (P(("blk", "qsub"), None), P("blk", None), P(("blk", "qsub")), P(("blk", "qsub")))
    return jax.shard_map(body, mesh=mesh, in_specs=in_specs, out_specs=P("blk"), check_vma=False)
```
